32 devices in a mesh: groups: 2 (over y), row: 4 (over z), col: 2 (over x), mode: 2 (over core).
Axes of the slice: x: 2, y: 2, z: 4, core: 2. Of those that a mesh axis runs over, the one named last changes fastest.
Arguments:
- object_field: float32 [2048, 2, 1024], P(('groups', 'row'), None, 'col'), parts along dimension 0, may hold values from -12 to 12
- probe_field: float32 [512, 2, 256], P('groups'), parts along dimension 0, may hold values from -5 to 5
- amplitudes: bfloat16 [128, 256, 256], P(('groups', 'row', 'col', 'mode')), parts along dimension 0
- row_offset: int32 [128], P(('groups', 'row', 'col', 'mode')), parts along dimension 0, may hold values from 0 to 768, as said below
- col_offset: int32 [128], P(('groups', 'row', 'col', 'mode')), parts along dimension 0, may hold values from 0 to 768, as said below
- counts: int32 [32], P(('groups', 'row', 'col', 'mode')), parts along dimension 0, may hold values from 1 to 4
Outputs:
- object_new: float32 [2048, 2, 1024], P(('groups', 'row', 'mode'), None, 'col'), parts along dimension 0
- probe_new: float32 [512, 2, 256], P('groups'), parts along dimension 0
The draws below stay inside these ranges and needn't reach their ends.
There are 2 independent parts, one for each index of `groups`. The reference program is written for one: setup_inputs(seed, part) draws one part's arguments, and reference() takes and returns one part's arrays. A program takes and returns all parts, laid end to end along the dimension named above; each array names one. Nothing has to cross between parts.
Inputs may be any that keep to these rules, and one draw needn't show every extreme that they name: `row_offset`: slot j lies on device j div 4 of row+col+mode; its patch starts inside that device's object tile of 256 rows, on a multiple of 64, and stays inside the object. `col_offset`: its patch starts inside the device's tile of 512 columns, on a multiple of 64, and stays inside the object.
All inputs are finite; a program needn't handle non-finite values.
Results may differ from the reference program's by a relative error of at most 0.0007.
The reference program's roundings to bfloat16 on the way count: a program that leaves them out, or rounds other values in their place, can miss the bound.
Values may be sent and summed in bfloat16 or wider, within the bound.
No kernel may reach another device: no remote copies, remote signals or barrier semaphores. Data moves between devices by JAX's collectives and lax.ppermute only.
A program may use at most 64 MiB of HBM per device.

```python
import math
import jax
import jax.numpy as jnp
from jax import lax

FRAME = 256
TILE_R = 256
TILE_C = 512
POS_DEV = 4
OBJ_R = 1024
OBJ_C = 1024
DEV_PART = 16
POSITIONS = 64


def offsets_within(key, device_ids, slot_within, tile_ids, tiles_count, extent):
    raster_step = FRAME // 4
    limit = jnp.where(tile_ids == tiles_count - 1, extent - FRAME + 1, extent).astype(jnp.int32)
    points = ((limit - 1) // raster_step + 1).astype(jnp.int32)
    raw_index = jax.random.randint(jax.random.fold_in(key, 1), device_ids.shape, 0, points).astype(jnp.int32)
    favored = jax.random.randint(jax.random.fold_in(key, 3), (), 0, 4).astype(jnp.int32)
    take_favored = jax.random.randint(jax.random.fold_in(key, 4), device_ids.shape, 0, 2) == 1
    aligned = favored + 4 * (raw_index // 4)
    index = jnp.where(take_favored & (aligned < points), aligned, raw_index)
    picks = jax.random.randint(jax.random.fold_in(key, 2), (DEV_PART,), 0, POS_DEV).astype(jnp.int32)
    chosen = picks[device_ids]
    index = jnp.where(slot_within == chosen, points - 1, index)
    index = jnp.where(slot_within == (chosen + 1) % POS_DEV, 0, index)
    return (tile_ids * extent + index * raster_step).astype(jnp.int32)


def draw_row_offset(key, part):
    slot_ids = jnp.arange(POSITIONS, dtype=jnp.int32)
    device_ids = slot_ids // POS_DEV
    rows_count = OBJ_R // TILE_R
    per_row = DEV_PART // rows_count
    tile_ids = device_ids // per_row
    return offsets_within(jax.random.fold_in(key, 11), device_ids, slot_ids % POS_DEV, tile_ids, rows_count, TILE_R)


def draw_col_offset(key, part):
    slot_ids = jnp.arange(POSITIONS, dtype=jnp.int32)
    device_ids = slot_ids // POS_DEV
    rows_count = OBJ_R // TILE_R
    cols_count = OBJ_C // TILE_C
    modes_count = DEV_PART // (rows_count * cols_count)
    tile_ids = device_ids // modes_count % cols_count
    return offsets_within(jax.random.fold_in(key, 12), device_ids, slot_ids % POS_DEV, tile_ids, cols_count, TILE_C)


def draw_counts(key, part):
    first_draw = jax.random.randint(jax.random.fold_in(key, 21), (DEV_PART,), 0, POS_DEV)
    second_draw = jax.random.randint(jax.random.fold_in(key, 22), (DEV_PART,), 0, POS_DEV)
    base_count = 1 + jnp.minimum(first_draw, second_draw)
    phase_pick = jax.random.randint(jax.random.fold_in(key, 23), (), 0, 8)
    device_ids = jnp.arange(DEV_PART, dtype=jnp.int32)
    return jnp.where(device_ids % 8 == phase_pick, POS_DEV, base_count).astype(jnp.int32)


def draw_amplitudes(key, part):
    position_frac = jnp.arange(POSITIONS, dtype=jnp.float32) / max(POSITIONS - 1, 1)
    frame_gain = jax.random.uniform(jax.random.fold_in(key, 31), (POSITIONS, 1, 1), minval=0.7, maxval=1.4)
    ramp_values = 1.0 + 2.0 * position_frac
    normal_values = jnp.clip(jax.random.normal(jax.random.fold_in(key, 33), (POSITIONS, FRAME, FRAME)), -5.0, 5.0)
    values = jnp.abs(normal_values) * 1.25
    return (values * frame_gain * ramp_values[:, None, None]).astype(jnp.bfloat16)


def draw_object_field(key, part):
    normal_values = jnp.clip(jax.random.normal(jax.random.fold_in(key, 41), (OBJ_R, 2, OBJ_C)), -5.0, 5.0) * 0.7
    return normal_values.astype(jnp.float32)


def noise(own_key, shape, deviation, bound, kind=jnp.bfloat16):
    entries = jax.random.normal(own_key, shape, jnp.float32) * deviation
    return jnp.minimum(jnp.maximum(entries, -bound), bound).astype(kind)


def setup_inputs(seed: int = 0, part: int = 0) -> dict:
    arg_keys = jax.random.split(jax.random.key(seed), 7)
    part_keys = jax.random.split(jax.random.fold_in(arg_keys[6], part), 7)
    return {
        "object_field": draw_object_field(jax.random.fold_in(jax.random.fold_in(arg_keys[6], part), 71), part),
        "probe_field": noise(part_keys[1], (FRAME, 2, FRAME), 0.7, 5.0, jnp.float32),
        "amplitudes": draw_amplitudes(jax.random.fold_in(jax.random.fold_in(arg_keys[6], part), 71), part),
        "row_offset": draw_row_offset(jax.random.fold_in(jax.random.fold_in(arg_keys[6], part), 71), part),
        "col_offset": draw_col_offset(jax.random.fold_in(jax.random.fold_in(arg_keys[6], part), 71), part),
        "counts": draw_counts(jax.random.fold_in(jax.random.fold_in(arg_keys[6], part), 71), part),
    }


MODULUS_FLOOR = 0.5
EPSILON = 1e-05
REGULARIZER = 1.0

def dft_table(points, sign):
    freq_index = jnp.arange(points, dtype=jnp.int32)
    product = freq_index[:, None] * freq_index[None, :] % points
    angle_grid = 2.0 * math.pi / points * product.astype(jnp.float32)
    norm_factor = 1.0 / math.sqrt(points)
    cosine = jnp.cos(angle_grid) * norm_factor
    sine_part = jnp.sin(angle_grid) * (sign * norm_factor)
    upper_rows = jnp.stack([cosine, sine_part], axis=-1)
    lower_rows = jnp.stack([-sine_part, cosine], axis=-1)
    return jnp.stack([upper_rows, lower_rows], axis=1).astype(jnp.bfloat16)

def transform(frames, dft_matrix):
    wide_table = dft_matrix.astype(jnp.float32)
    frames = lax.optimization_barrier(frames)
    first_pass = jnp.einsum('kanb,nbm->kam', wide_table, frames.astype(jnp.float32), precision=lax.Precision.HIGHEST)
    first_pass = lax.optimization_barrier(first_pass.astype(jnp.bfloat16)).astype(jnp.float32)
    return jnp.einsum('kbm,lamb->kal', first_pass, wide_table, precision=lax.Precision.HIGHEST)

def frame_update(obj_patch, probe_field, amplitude, forward, inverse):
    obj_re = obj_patch[:, 0, :].astype(jnp.float32)
    obj_im = obj_patch[:, 1, :].astype(jnp.float32)
    probe_re = probe_field[:, 0, :]
    probe_im = probe_field[:, 1, :]
    exit_wave = jnp.stack([probe_re * obj_re - probe_im * obj_im, probe_re * obj_im + probe_im * obj_re], axis=1).astype(jnp.bfloat16)
    far_field = transform(exit_wave, forward)
    modulus = jnp.sqrt(far_field[:, 0, :] ** 2 + far_field[:, 1, :] ** 2)
    factor = amplitude.astype(jnp.float32) / jnp.maximum(modulus, MODULUS_FLOOR) - 1.0
    change = (far_field * factor[:, None, :]).astype(jnp.bfloat16)
    back_field = transform(change, inverse)
    chi_re = back_field[:, 0, :]
    chi_im = back_field[:, 1, :]
    obj_step = jnp.stack([probe_re * chi_re + probe_im * chi_im, probe_re * chi_im - probe_im * chi_re], axis=1)
    grad_re = obj_re * chi_re + obj_im * chi_im
    grad_im = obj_re * chi_im - obj_im * chi_re
    weight = obj_re * obj_re + obj_im * obj_im
    return (obj_step, grad_re, grad_im, weight)

def reference(object_field, probe_field, amplitudes, row_offset, col_offset, counts):
    forward = dft_table(FRAME, 1.0)
    inverse = dft_table(FRAME, -1.0)
    object_half = lax.optimization_barrier(object_field.astype(jnp.bfloat16))
    slot_ids = jnp.arange(POSITIONS, dtype=jnp.int32)
    live_mask = (slot_ids % POS_DEV < counts[slot_ids // POS_DEV]).astype(jnp.float32)

    def scan_step(state_now, scan_item):
        update_sum, grad_re, grad_im, weight_sum = state_now
        amplitude, top_row, left_col, live_flag = scan_item
        start = (top_row.astype(jnp.int32), jnp.int32(0), left_col.astype(jnp.int32))
        obj_patch = lax.dynamic_slice(object_half, start, (FRAME, 2, FRAME))
        obj_step, part_re, part_im, weight = frame_update(obj_patch, probe_field, amplitude, forward, inverse)
        current = lax.dynamic_slice(update_sum, start, (FRAME, 2, FRAME))
        update_sum = lax.dynamic_update_slice(update_sum, current + live_flag * obj_step, start)
        return ((update_sum, grad_re + live_flag * part_re, grad_im + live_flag * part_im, weight_sum + live_flag * weight), None)
    zero_frame = jnp.zeros((FRAME, FRAME), jnp.float32)
    initial = (jnp.zeros(object_field.shape, jnp.float32), zero_frame, zero_frame, zero_frame)
    final_state, _ = lax.scan(scan_step, initial, (amplitudes, row_offset, col_offset, live_mask))
    update_sum, grad_re, grad_im, weight_sum = final_state
    probe_peak = jnp.max(probe_field[:, 0, :] ** 2 + probe_field[:, 1, :] ** 2) + EPSILON
    object_new = object_field + update_sum / probe_peak
    denominator = weight_sum + REGULARIZER
    probe_new = probe_field + jnp.stack([grad_re / denominator, grad_im / denominator], axis=1)
    return (object_new, probe_new)
```

```python
import math

import jax
import jax.numpy as jnp
import numpy as np
from jax import lax
from jax.experimental import pallas as pl
from jax.experimental.pallas import tpu as pltpu
from jax.sharding import PartitionSpec as P

MODULUS_FLOOR = 0.5
EPSILON = 1e-05
REGULARIZER = 1.0
STEP = 64
LANES = 128
PAD = 16
BITS = 14
CHUNK = 32

F32 = jnp.float32
BF16 = jnp.bfloat16
I16 = jnp.int16


def dft_tables(points):
    index = np.arange(points)
    product = (index[:, None] * index[None, :]) % points
    angle = np.float32(2.0 * math.pi / points) * product.astype(np.float32)
    norm = 1.0 / math.sqrt(points)
    cosine = (np.cos(angle) * np.float32(norm)).astype(np.float32)
    sine = (np.sin(angle) * np.float32(norm)).astype(np.float32)
    plus = np.block([[cosine, sine], [-sine, cosine]])
    minus = np.block([[cosine, -sine], [sine, cosine]])
    return jnp.asarray(plus, BF16), jnp.asarray(minus, BF16)


def vmem_call(kernel, outs, *operands, smem=0, scratch=(), flops=0, name=None):
    specs = [pl.BlockSpec(memory_space=pltpu.SMEM)] * smem
    specs += [pl.BlockSpec(memory_space=pltpu.VMEM)] * (len(operands) - smem)
    moved = sum(math.prod(o.shape) * o.dtype.itemsize for o in (*operands, *outs))
    return pl.pallas_call(
        kernel,
        out_shape=tuple(jax.ShapeDtypeStruct(o.shape, o.dtype) for o in outs),
        in_specs=specs,
        out_specs=tuple(pl.BlockSpec(memory_space=pltpu.VMEM) for _ in outs),
        scratch_shapes=scratch,
        compiler_params=pltpu.CompilerParams(vmem_limit_bytes=40 * 1024 * 1024),
        cost_estimate=pl.CostEstimate(flops=flops, bytes_accessed=moved, transcendentals=0),
        name=name,
    )(*operands)


def shape(dims, dtype):
    return jax.ShapeDtypeStruct(dims, dtype)


def encode(block):
    peak = jnp.max(jnp.abs(block), axis=0, keepdims=True)
    power = jnp.ceil(jnp.log2(jnp.maximum(peak, 1e-30)))
    whole = jnp.round(block * jnp.exp2(BITS - power))
    decoded = whole * jnp.exp2(power - BITS)
    tail = jnp.broadcast_to(power, (PAD, block.shape[1]))
    return whole.astype(jnp.int32).astype(I16), tail.astype(jnp.int32).astype(I16), decoded


def encode_to(ref, plane, block):
    rows = block.shape[0]
    code, tail, decoded = encode(block)
    ref[plane, :rows, :] = code
    ref[plane, rows:, :] = tail
    return decoded


def decode(ref, plane):
    rows = ref.shape[1] - PAD
    power = ref[plane, rows:, :].astype(jnp.int32).astype(F32)[:1]
    return ref[plane, :rows, :].astype(jnp.int32).astype(F32) * jnp.exp2(power - BITS)


def frames_kernel(
    row_ref, col_ref, count_ref, own_ref, a_recv, a_swap, d_recv, d_swap, probe_ref, amp_ref, plus_ref, minus_ref,
    keep_ref, send_ref, gkeep_ref, gsend_ref,
    ext, patch, wave, half, field, total, grads,
):
    _, tile_rows, tile_cols = own_ref.shape
    frame = probe_ref.shape[1]
    halo = a_recv.shape[1]
    mode = lax.axis_index("mode")
    top = lax.axis_index("row") * tile_rows
    left = lax.axis_index("col") * tile_cols
    part = halo // 2

    ext[:, :tile_rows, :tile_cols] = own_ref[...]

    def place(below, right, diag0, diag1):
        ext[:, tile_rows:, :tile_cols] = below[...]
        ext[:, : tile_rows // 2, tile_cols:] = right[:, : tile_rows // 2, :frame]
        ext[:, tile_rows // 2 : tile_rows, tile_cols:] = right[:, : tile_rows // 2, frame:]
        ext[:, tile_rows : tile_rows + part, tile_cols:] = diag0[...]
        ext[:, tile_rows + part :, tile_cols:] = diag1[...]

    @pl.when(mode == 0)
    def _():
        place(a_recv, a_swap, d_recv, d_swap)

    @pl.when(mode == 1)
    def _():
        place(a_swap, a_recv, d_swap, d_recv)

    total[...] = jnp.zeros(total.shape, F32)
    grads[...] = jnp.zeros(grads.shape, F32)
    tiles = frame // LANES
    low = lax.broadcasted_iota(jnp.int32, (CHUNK, LANES), 1) < STEP

    def turned(value):
        return pltpu.roll(value, STEP, 1)

    def one(position, carry):
        row = pl.multiple_of(row_ref[position] - top, STEP)
        shift = col_ref[position] - left
        odd = (shift // STEP) % 2 == 1
        base = pl.multiple_of((shift // LANES) * LANES, LANES)

        for start in range(0, frame, CHUNK):
            rows = pl.ds(start, CHUNK)
            obj = []
            for plane in range(2):
                got = ext[plane, pl.ds(pl.multiple_of(row + start, CHUNK), CHUNK), pl.ds(base, frame + LANES)].astype(F32)
                pieces = [got[:, t * LANES : (t + 1) * LANES] for t in range(tiles + 1)]
                rolled = [turned(piece) for piece in pieces]
                chosen = [
                    jnp.where(odd, jnp.where(low, rolled[t], rolled[t + 1]), pieces[t]) for t in range(tiles)
                ]
                obj.append(jnp.concatenate(chosen, axis=1))
                patch[plane, rows, :] = obj[plane]
            p_re, p_im = probe_ref[0, rows, :], probe_ref[1, rows, :]
            wave[rows, :] = (p_re * obj[0] - p_im * obj[1]).astype(BF16)
            wave[pl.ds(frame + start, CHUNK), :] = (p_re * obj[1] + p_im * obj[0]).astype(BF16)

        def transform(left_table, right_table):
            first = jnp.dot(left_table[...], wave[...], preferred_element_type=F32)
            half[:, :frame] = first[:frame].astype(BF16)
            half[:, frame:] = first[frame:].astype(BF16)
            field[...] = jnp.dot(half[...], right_table[...], preferred_element_type=F32)

        transform(plus_ref, minus_ref)
        for start in range(0, frame, CHUNK):
            rows = pl.ds(start, CHUNK)
            re, im = field[rows, :frame], field[rows, frame:]
            inverse = jnp.minimum(lax.rsqrt(re * re + im * im), 1.0 / MODULUS_FLOOR)
            factor = amp_ref[position, rows, :].astype(F32) * inverse - 1.0
            wave[rows, :] = (re * factor).astype(BF16)
            wave[pl.ds(frame + start, CHUNK), :] = (im * factor).astype(BF16)
        transform(minus_ref, plus_ref)
        for start in range(0, frame, CHUNK):
            rows = pl.ds(start, CHUNK)
            re, im = field[rows, :frame], field[rows, frame:]
            p_re, p_im = probe_ref[0, rows, :], probe_ref[1, rows, :]
            o_re, o_im = patch[0, rows, :], patch[1, rows, :]
            steps = (p_re * re + p_im * im, p_re * im - p_im * re)
            for plane in range(2):
                pieces = [steps[plane][:, t * LANES : (t + 1) * LANES] for t in range(tiles)]
                rolled = [turned(piece) for piece in pieces]
                zero = jnp.zeros_like(pieces[0])
                moved = []
                for t in range(tiles + 1):
                    before = rolled[t - 1] if t > 0 else zero
                    here = rolled[t] if t < tiles else zero
                    moved.append(
                        jnp.where(odd, jnp.where(low, before, here), pieces[t] if t < tiles else zero)
                    )
                where = (plane, pl.ds(pl.multiple_of(row + start, CHUNK), CHUNK), pl.ds(base, frame + LANES))
                total[where] += jnp.concatenate(moved, axis=1)
            grads[0, rows, :] += o_re * re + o_im * im
            grads[1, rows, :] += o_re * im - o_im * re
            grads[2, rows, :] += o_re * o_re + o_im * o_im
        return carry

    lax.fori_loop(0, count_ref[0], one, 0)

    part_rows = tile_rows // 2
    part_frame = frame // 2
    for target, gtarget, who in ((keep_ref, gkeep_ref, mode), (send_ref, gsend_ref, 1 - mode)):
        target[:, :part_rows, :] = total[:, pl.ds(pl.multiple_of(who * part_rows, part_rows), part_rows), :]
        target[:, part_rows:, :] = total[:, pl.ds(pl.multiple_of(tile_rows + who * part, 32), part), :]
        gtarget[...] = grads[:, pl.ds(pl.multiple_of(who * part_frame, part_frame), part_frame), :]


def after_mode_kernel(keep, recv, gkeep, grecv, own_ref, xsend_ref, g_ref, gsend_ref):
    cols = own_ref.shape[2]
    for plane in range(2):
        own_ref[plane] = keep[plane, :, :cols] + recv[plane, :, :cols]
        encode_to(xsend_ref, plane, keep[plane, :, cols:] + recv[plane, :, cols:])
    for plane in range(3):
        g_ref[plane] = encode_to(gsend_ref, plane, gkeep[plane] + grecv[plane])


def grad_step(g, grecv, g_ref, gsend_ref):
    for plane in range(3):
        g_ref[plane] = encode_to(gsend_ref, plane, g[plane] + decode(grecv, plane))


def after_first_kernel(own, xrecv, g, grecv, tile_ref, rowsend_ref, g_ref, gsend_ref):
    rows = tile_ref.shape[1]
    frame = xrecv.shape[2]
    for plane in range(2):
        got = decode(xrecv, plane)
        tile_ref[plane, :, :frame] = own[plane, :rows, :frame] + got[:rows]
        tile_ref[plane, :, frame:] = own[plane, :rows, frame:]
        low = jnp.concatenate([own[plane, rows:, :frame] + got[rows:], own[plane, rows:, frame:]], axis=1)
        encode_to(rowsend_ref, plane, low)
    grad_step(g, grecv, g_ref, gsend_ref)


def after_second_kernel(tile, rowrecv, g, grecv, tile_ref, spill_ref, g_ref, gsend_ref):
    mode = lax.axis_index("mode")
    part = rowrecv.shape[1] - PAD
    over = tile.shape[1] - part
    for plane in range(2):
        got = decode(rowrecv, plane)
        tile_ref[plane] = tile[plane]
        spill_ref[plane] = got[:over]

        @pl.when(mode == 0)
        def _(plane=plane, got=got):
            tile_ref[plane, :part, :] += got

        @pl.when(mode == 1)
        def _(plane=plane, got=got):
            tile_ref[plane, : part - over, :] += got[over:]

    grad_step(g, grecv, g_ref, gsend_ref)


def grad_only_kernel(g, grecv, g_ref, gsend_ref):
    grad_step(g, grecv, g_ref, gsend_ref)


def probe_kernel(g, grecv, step_ref):
    sums = [g[plane] + decode(grecv, plane) for plane in range(3)]
    for plane in range(2):
        step_ref[plane] = sums[plane] / (sums[2] + REGULARIZER)


def moved_along(value, axis, steps):
    count = lax.axis_size(axis)
    first, last = (max(0, -steps), min(count, count - steps))
    return lax.ppermute(value, axis, [(source, source + steps) for source in range(first, last)])


def swapped(value, axis, distance):
    count = lax.axis_size(axis)
    return lax.ppermute(value, axis, [(source, source ^ distance) for source in range(count)])


def body(object_field, probe_field, amplitudes, row_offset, col_offset, counts):
    tile_rows, _, tile_cols = object_field.shape
    frame = probe_field.shape[0]
    halo = frame - STEP
    part = halo // 2
    rows_count, cols_count = lax.axis_size("row"), lax.axis_size("col")
    mode = lax.axis_index("mode")
    plus, minus = dft_tables(frame)

    own = jnp.transpose(object_field.astype(BF16), (1, 0, 2))
    mid = tile_rows // 2
    columns = jnp.concatenate([own[:, :mid, :frame], own[:, mid:, :frame]], axis=2)
    columns = jnp.pad(columns, ((0, 0), (0, halo - mid), (0, 0)))
    a_send = jnp.where(mode == 0, own[:, :halo], columns)
    d_send = jnp.where(mode == 0, own[:, :part, :frame], own[:, part:halo, :frame])
    a_pairs, d_pairs = [], []
    for r in range(rows_count):
        for c in range(cols_count):
            here = (r * cols_count + c) * 2
            if r > 0:
                a_pairs.append((here, here - cols_count * 2))
            if c > 0:
                a_pairs.append((here + 1, here + 1 - 2))
            if r > 0 and c > 0:
                d_pairs += [(here + m, here + m - cols_count * 2 - 2) for m in range(2)]
    axes = ("row", "col", "mode")
    a_recv = lax.ppermute(a_send, axes, a_pairs)
    d_recv = lax.ppermute(d_send, axes, d_pairs)
    a_swap = swapped(a_recv, "mode", 1)
    d_swap = swapped(d_recv, "mode", 1)
    probe = jnp.transpose(probe_field, (1, 0, 2))

    ext_rows, ext_cols = tile_rows + halo, tile_cols + frame
    held = mid + part
    u_shape = shape((2, held, ext_cols), F32)
    g_shape = shape((3, frame // 2, frame), F32)
    g_code = shape((3, frame // 2 + PAD, frame), I16)
    keep, send, gkeep, gsend = vmem_call(
        frames_kernel,
        (u_shape, u_shape, g_shape, g_shape),
        row_offset, col_offset, counts, own, a_recv, a_swap, d_recv, d_swap, probe, amplitudes, plus, minus,
        smem=3,
        scratch=[
            pltpu.VMEM((2, ext_rows, ext_cols), BF16),
            pltpu.VMEM((2, frame, frame), F32),
            pltpu.VMEM((2 * frame, frame), BF16),
            pltpu.VMEM((frame, 2 * frame), BF16),
            pltpu.VMEM((frame, 2 * frame), F32),
            pltpu.VMEM((2, ext_rows, ext_cols), F32),
            pltpu.VMEM((3, frame, frame), F32),
        ],
        flops=4 * 32 * frame**3,
        name="frames",
    )
    recv = swapped(send, "mode", 1)
    grecv = swapped(gsend, "mode", 1)
    own_sum, xsend, g, gcode = vmem_call(
        after_mode_kernel,
        (shape((2, held, tile_cols), F32), shape((2, held + PAD, frame), I16), g_shape, g_code),
        keep, recv, gkeep, grecv, name="after_mode",
    )

    row_steps = [1 << k for k in range(rows_count.bit_length() - 1)]
    col_steps = [1 << k for k in range(cols_count.bit_length() - 1)]
    exchanges = [("row", row_steps[0]), ("col", col_steps[0])]
    exchanges += [("row", s) for s in row_steps[1:]] + [("col", s) for s in col_steps[1:]]

    xrecv = moved_along(xsend, "col", 1)
    gother = swapped(gcode, *exchanges[0])
    tile, rowsend, g, gcode = vmem_call(
        after_first_kernel,
        (shape((2, mid, tile_cols), F32), shape((2, part + PAD, tile_cols), I16), g_shape, g_code),
        own_sum, xrecv, g, gother, name="after_first",
    )
    rowrecv = moved_along(rowsend, "row", 1)
    gother = swapped(gcode, *exchanges[1])
    tile, spill, g, gcode = vmem_call(
        after_second_kernel,
        (shape((2, mid, tile_cols), F32), shape((2, mid - part, tile_cols), F32), g_shape, g_code),
        tile, rowrecv, g, gother, name="after_second",
    )
    for exchange in exchanges[2:-1]:
        gother = swapped(gcode, *exchange)
        g, gcode = vmem_call(grad_only_kernel, (g_shape, g_code), g, gother, name="grad_only")
    gother = swapped(gcode, *exchanges[-1])

    spilled = lax.ppermute(spill, "mode", [(1, 0)])
    tile = jnp.concatenate([tile[:, :part], tile[:, part:] + spilled], axis=1)
    rows_here = lax.dynamic_slice_in_dim(object_field, mode * mid, mid, 0)
    probe_peak = jnp.max(probe_field[:, 0, :] ** 2 + probe_field[:, 1, :] ** 2) + EPSILON
    object_new = rows_here + jnp.transpose(tile, (1, 0, 2)) / probe_peak

    (step,) = vmem_call(probe_kernel, (shape((2, frame // 2, frame), F32),), g, gother, name="probe")
    other = swapped(step, "mode", 1)
    first = jnp.where(mode == 0, step, other)
    second = jnp.where(mode == 0, other, step)
    probe_new = probe_field + jnp.transpose(jnp.concatenate([first, second], axis=1), (1, 0, 2))
    return (object_new, probe_new)


def solution(mesh):
    placed = (
        P(("groups", "row"), None, "col"),
        P("groups", None, None),
        P(("groups", "row", "col", "mode"), None, None),
        P(("groups", "row", "col", "mode")),
        P(("groups", "row", "col", "mode")),
        P(("groups", "row", "col", "mode")),
    )
    return jax.shard_map(
        body,
        mesh=mesh,
        in_specs=placed,
        out_specs=(P(("groups", "row", "mode"), None, "col"), P("groups", None, None)),
        check_vma=False,
    )
```

```python
import math

import jax
import jax.numpy as jnp
import numpy as np
from jax import lax
from jax.experimental import pallas as pl
from jax.experimental.pallas import tpu as pltpu
from jax.sharding import PartitionSpec as P

MODULUS_FLOOR = 0.5
EPSILON = 1e-05
REGULARIZER = 1.0
STEP = 64
LANES = 128
PAD = 16
BITS = 14
CHUNK = 32

F32 = jnp.float32
BF16 = jnp.bfloat16
I16 = jnp.int16


def dft_tables(points):
    index = np.arange(points)
    product = (index[:, None] * index[None, :]) % points
    angle = np.float32(2.0 * math.pi / points) * product.astype(np.float32)
    norm = 1.0 / math.sqrt(points)
    cosine = (np.cos(angle) * np.float32(norm)).astype(np.float32)
    sine = (np.sin(angle) * np.float32(norm)).astype(np.float32)
    plus = np.block([[cosine, sine], [-sine, cosine]])
    minus = np.block([[cosine, -sine], [sine, cosine]])
    return jnp.asarray(plus, BF16), jnp.asarray(minus, BF16)


def vmem_call(kernel, outs, *operands, smem=0, scratch=(), flops=0, name=None):
    specs = [pl.BlockSpec(memory_space=pltpu.SMEM)] * smem
    specs += [pl.BlockSpec(memory_space=pltpu.VMEM)] * (len(operands) - smem)
    moved = sum(math.prod(o.shape) * o.dtype.itemsize for o in (*operands, *outs))
    return pl.pallas_call(
        kernel,
        out_shape=tuple(jax.ShapeDtypeStruct(o.shape, o.dtype) for o in outs),
        in_specs=specs,
        out_specs=tuple(pl.BlockSpec(memory_space=pltpu.VMEM) for _ in outs),
        scratch_shapes=scratch,
        compiler_params=pltpu.CompilerParams(vmem_limit_bytes=40 * 1024 * 1024),
        cost_estimate=pl.CostEstimate(flops=flops, bytes_accessed=moved, transcendentals=0),
        name=name,
    )(*operands)


def shape(dims, dtype):
    return jax.ShapeDtypeStruct(dims, dtype)


def encode(block):
    peak = jnp.max(jnp.abs(block), axis=0, keepdims=True)
    power = jnp.ceil(jnp.log2(jnp.maximum(peak, 1e-30)))
    whole = jnp.round(block * jnp.exp2(BITS - power))
    return whole.astype(jnp.int32).astype(I16), power, whole * jnp.exp2(power - BITS)


def encode_to(ref, blocks):
    rows, cols = blocks[0].shape
    tail = jnp.zeros((PAD, cols), F32)
    row = lax.broadcasted_iota(jnp.int32, (PAD, cols), 0)
    decoded = []
    for n, block in enumerate(blocks):
        code, power, back = encode(block)
        ref[n * rows : (n + 1) * rows, :] = code
        tail = jnp.where(row == n, power, tail)
        decoded.append(back)
    ref[len(blocks) * rows :, :] = tail.astype(jnp.int32).astype(I16)
    return decoded


def decode(ref, count):
    rows = (ref.shape[0] - PAD) // count
    tail = ref[count * rows :, :].astype(jnp.int32).astype(F32)
    return [
        ref[n * rows : (n + 1) * rows, :].astype(jnp.int32).astype(F32) * jnp.exp2(tail[n : n + 1] - BITS)
        for n in range(count)
    ]


def turned(value):
    return pltpu.roll(value, STEP, 1)


def low_lanes(rows):
    return lax.broadcasted_iota(jnp.int32, (rows, LANES), 1) < STEP


def folded(first, second):
    mid = first.shape[0] // 2
    return jnp.concatenate([first, jnp.where(low_lanes(mid), second[:mid], turned(second[mid:]))], axis=0)


def unfolded(block):
    rows = block.shape[0] * 2 // 3
    tail, low = block[rows:], low_lanes(rows // 2)
    zero = jnp.zeros_like(tail)
    second = jnp.concatenate([jnp.where(low, tail, zero), jnp.where(low, turned(tail), zero)], axis=0)
    return jnp.concatenate([block[:rows], second], axis=1)


def frames_kernel(
    row_ref, col_ref, count_ref, own_ref, r_mine, r_other, x_mine, x_other, d_mine, d_other,
    probe_ref, amp_ref, plus_ref, minus_ref,
    lkeep_ref, lsend_ref, rkeep_ref, rsend_ref, gkeep_ref, gsend_ref, peak_ref,
    ext, patch, wave, half, field, total, grads,
):
    _, tile_rows, tile_cols = own_ref.shape
    frame = probe_ref.shape[1]
    part = r_mine.shape[1]
    mid = tile_rows // 2
    mode = lax.axis_index("mode")
    top = lax.axis_index("row") * tile_rows
    left = lax.axis_index("col") * tile_cols

    ext[:, :tile_rows, :tile_cols] = own_ref[...]
    for who, below, right, diagonal in ((mode, r_mine, x_mine, d_mine), (1 - mode, r_other, x_other, d_other)):
        rows = pl.ds(pl.multiple_of(tile_rows + who * part, 32), part)
        ext[:, rows, :tile_cols] = below[...]
        ext[:, rows, tile_cols:] = diagonal[...]
        ext[:, pl.ds(pl.multiple_of(who * mid, mid), mid), tile_cols:] = right[...]

    power = probe_ref[0] * probe_ref[0] + probe_ref[1] * probe_ref[1]
    peak_ref[...] = jnp.broadcast_to(jnp.max(power, keepdims=True), peak_ref.shape) + EPSILON

    total[...] = jnp.zeros(total.shape, F32)
    grads[...] = jnp.zeros(grads.shape, F32)
    tiles = frame // LANES
    low = low_lanes(CHUNK)

    def one(position, carry):
        row = pl.multiple_of(row_ref[position] - top, STEP)
        shift = col_ref[position] - left
        odd = (shift // STEP) % 2 == 1
        base = pl.multiple_of((shift // LANES) * LANES, LANES)

        for start in range(0, frame, CHUNK):
            rows = pl.ds(start, CHUNK)
            obj = []
            for plane in range(2):
                got = ext[plane, pl.ds(pl.multiple_of(row + start, CHUNK), CHUNK), pl.ds(base, frame + LANES)].astype(F32)
                pieces = [got[:, t * LANES : (t + 1) * LANES] for t in range(tiles + 1)]
                rolled = [turned(piece) for piece in pieces]
                chosen = [
                    jnp.where(odd, jnp.where(low, rolled[t], rolled[t + 1]), pieces[t]) for t in range(tiles)
                ]
                obj.append(jnp.concatenate(chosen, axis=1))
                patch[plane, rows, :] = obj[plane]
            p_re, p_im = probe_ref[0, rows, :], probe_ref[1, rows, :]
            wave[rows, :] = (p_re * obj[0] - p_im * obj[1]).astype(BF16)
            wave[pl.ds(frame + start, CHUNK), :] = (p_re * obj[1] + p_im * obj[0]).astype(BF16)

        def transform(left_table, right_table):
            first = jnp.dot(left_table[...], wave[...], preferred_element_type=F32)
            half[:, :frame] = first[:frame].astype(BF16)
            half[:, frame:] = first[frame:].astype(BF16)
            field[...] = jnp.dot(half[...], right_table[...], preferred_element_type=F32)

        transform(plus_ref, minus_ref)
        for start in range(0, frame, CHUNK):
            rows = pl.ds(start, CHUNK)
            re, im = field[rows, :frame], field[rows, frame:]
            inverse = jnp.minimum(lax.rsqrt(re * re + im * im), 1.0 / MODULUS_FLOOR)
            factor = amp_ref[position, rows, :].astype(F32) * inverse - 1.0
            wave[rows, :] = (re * factor).astype(BF16)
            wave[pl.ds(frame + start, CHUNK), :] = (im * factor).astype(BF16)
        transform(minus_ref, plus_ref)
        for start in range(0, frame, CHUNK):
            rows = pl.ds(start, CHUNK)
            re, im = field[rows, :frame], field[rows, frame:]
            p_re, p_im = probe_ref[0, rows, :], probe_ref[1, rows, :]
            o_re, o_im = patch[0, rows, :], patch[1, rows, :]
            steps = (p_re * re + p_im * im, p_re * im - p_im * re)
            for plane in range(2):
                pieces = [steps[plane][:, t * LANES : (t + 1) * LANES] for t in range(tiles)]
                rolled = [turned(piece) for piece in pieces]
                zero = jnp.zeros_like(pieces[0])
                moved = []
                for t in range(tiles + 1):
                    before = rolled[t - 1] if t > 0 else zero
                    here = rolled[t] if t < tiles else zero
                    moved.append(
                        jnp.where(odd, jnp.where(low, before, here), pieces[t] if t < tiles else zero)
                    )
                where = (plane, pl.ds(pl.multiple_of(row + start, CHUNK), CHUNK), pl.ds(base, frame + LANES))
                total[where] += jnp.concatenate(moved, axis=1)
            grads[0, rows, :] += o_re * re + o_im * im
            grads[1, rows, :] += o_re * im - o_im * re
            grads[2, rows, :] += o_re * o_re + o_im * o_im
        return carry

    lax.fori_loop(0, count_ref[0], one, 0)

    part_frame = frame // 2
    for who, l_ref, r_ref, g_ref in ((1 - mode, lsend_ref, rsend_ref, gsend_ref), (mode, lkeep_ref, rkeep_ref, gkeep_ref)):
        upper = pl.ds(pl.multiple_of(who * mid, mid), mid)
        lower = pl.ds(pl.multiple_of(tile_rows + who * part, 32), part)
        l_ref[:, :mid, :] = total[:, upper, :tile_cols]
        l_ref[:, mid:, :] = total[:, lower, :tile_cols]
        for plane in range(2):
            right = jnp.concatenate([total[plane, upper, tile_cols:], total[plane, lower, tile_cols:]], axis=0)
            r_ref[plane] = folded(right[:, :LANES], right[:, LANES:])
        g_ref[...] = grads[:, pl.ds(pl.multiple_of(who * part_frame, part_frame), part_frame), :]


def after_mode_kernel(rkeep, rrecv, gkeep, grecv, xsend_ref, g_ref, gsend_ref, w_ref, wsend_ref):
    encode_to(xsend_ref, [rkeep[plane] + rrecv[plane] for plane in range(2)])
    sums = [gkeep[plane] + grecv[plane] for plane in range(3)]
    g_ref[0], g_ref[1] = encode_to(gsend_ref, sums[:2])
    (w_ref[...],) = encode_to(wsend_ref, sums[2:])


def joined_kernel(g, grecv, w, wrecv, sums_ref, send_ref):
    got = decode(grecv, 2)
    sums = [g[plane] + got[plane] for plane in range(2)] + [w[...] + decode(wrecv, 1)[0]]
    sums_ref[0], sums_ref[1], sums_ref[2] = encode_to(send_ref, sums)


def split_kernel(sums, recv, g_ref, gsend_ref, w_ref, wsend_ref):
    total = [sums[plane] + got for plane, got in enumerate(decode(recv, 3))]
    g_ref[0], g_ref[1] = encode_to(gsend_ref, total[:2])
    (w_ref[...],) = encode_to(wsend_ref, total[2:])


def again_kernel(sums, recv, sums_ref, send_ref):
    total = [sums[plane] + got for plane, got in enumerate(decode(recv, 3))]
    sums_ref[0], sums_ref[1], sums_ref[2] = encode_to(send_ref, total)


def from_left_kernel(lkeep, lrecv, xrecv, tile_ref, rowsend_ref):
    rows = tile_ref.shape[1]
    came = jnp.where(lax.axis_index("col") > 0, 1.0, 0.0)
    below = []
    for plane, code in enumerate(decode(xrecv, 2)):
        got = unfolded(code) * came
        frame = got.shape[1]
        tile_ref[plane, :, :frame] = lkeep[plane, :rows, :frame] + lrecv[plane, :rows, :frame] + got[:rows]
        tile_ref[plane, :, frame:] = lkeep[plane, :rows, frame:] + lrecv[plane, :rows, frame:]
        near = lkeep[plane, rows:, :frame] + lrecv[plane, rows:, :frame] + got[rows:]
        far = lkeep[plane, rows:, frame:] + lrecv[plane, rows:, frame:]
        below.append(jnp.concatenate([near, far], axis=1))
    encode_to(rowsend_ref, below)


def from_above_kernel(rowrecv, rows_ref, spill_ref):
    got = decode(rowrecv, 2)
    came = jnp.where(lax.axis_index("row") > 0, 1.0, 0.0)
    over = spill_ref.shape[1]
    for plane in range(2):
        rows_ref[plane] = got[plane] * came
        spill_ref[plane] = got[plane][:over] * came


def object_kernel(object_ref, tile, rows, spilled, peak, out_ref):
    mode = lax.axis_index("mode")
    mid, part = tile.shape[1], rows.shape[1]
    over = mid - part
    scale = 1.0 / peak[0:1, 0:1]
    for who in range(2):

        @pl.when(mode == who)
        def _(who=who):
            for plane in range(2):
                for start in range(0, mid, CHUNK):
                    step = tile[plane, start : start + CHUNK, :]
                    if who == 0:
                        step += rows[plane, start : start + CHUNK, :] if start < part else spilled[plane, start - part :, :]
                    elif start < part - over:
                        step += rows[plane, start + over : start + over + CHUNK, :]
                    old = object_ref[who * mid + start : who * mid + start + CHUNK, plane, :]
                    out_ref[start : start + CHUNK, plane, :] = old + step * scale


def probe_kernel(g, grecv, w, wrecv, step_ref):
    weight = w[...] + decode(wrecv, 1)[0] + REGULARIZER
    got = decode(grecv, 2)
    for plane in range(2):
        step_ref[plane] = (g[plane] + got[plane]) / weight


def probe_out_kernel(probe_ref, mine, other, out_ref):
    mode = lax.axis_index("mode")
    rows = mine.shape[1]
    for start in range(0, rows, CHUNK):
        for plane in range(2):
            one, two = mine[plane, start : start + CHUNK, :], other[plane, start : start + CHUNK, :]
            first, second = jnp.where(mode == 0, one, two), jnp.where(mode == 0, two, one)
            for place, step in ((start, first), (rows + start, second)):
                old = probe_ref[place : place + CHUNK, plane, :]
                out_ref[place : place + CHUNK, plane, :] = old + step


def moved_along(value, axis, steps):
    count = lax.axis_size(axis)
    if count == 2:
        return swapped(value, axis, 1)
    first, last = (max(0, -steps), min(count, count - steps))
    return lax.ppermute(value, axis, [(source, source + steps) for source in range(first, last)])


def swapped(value, axis, distance):
    count = lax.axis_size(axis)
    return lax.ppermute(value, axis, [(source, source ^ distance) for source in range(count)])


def body(object_field, probe_field, amplitudes, row_offset, col_offset, counts):
    tile_rows, _, tile_cols = object_field.shape
    frame = probe_field.shape[0]
    halo = frame - STEP
    part, mid = halo // 2, tile_rows // 2
    rows_count, cols_count = lax.axis_size("row"), lax.axis_size("col")
    mode = lax.axis_index("mode")
    plus, minus = dft_tables(frame)

    def planar(block):
        return jnp.transpose(block.astype(BF16), (1, 0, 2))

    r_send = planar(lax.dynamic_slice_in_dim(object_field, mode * part, part, 0))
    x_send = planar(lax.dynamic_slice_in_dim(object_field[:, :, :frame], mode * mid, mid, 0))
    r_send, x_send = lax.optimization_barrier((r_send, x_send))
    d_send = r_send[:, :, :frame]
    diagonal = []
    for r in range(1, rows_count):
        for c in range(1, cols_count):
            here = r * cols_count + c
            diagonal.append((here, here - cols_count - 1))
    r_mine = moved_along(r_send, "row", -1)
    d_mine = lax.ppermute(d_send, ("row", "col"), diagonal)
    x_mine = moved_along(x_send, "col", -1)
    r_mine, d_mine, x_mine = lax.optimization_barrier((r_mine, d_mine, x_mine))
    r_other, d_other, x_other = (swapped(v, "mode", 1) for v in (r_mine, d_mine, x_mine))
    own = planar(object_field)
    probe = jnp.transpose(probe_field, (1, 0, 2))

    held = mid + part
    l_shape = shape((2, held, tile_cols), F32)
    r_shape = shape((2, held * 3 // 2, LANES), F32)
    g_shape = shape((3, frame // 2, frame), F32)
    lkeep, lsend, rkeep, rsend, gkeep, gsend, peak = vmem_call(
        frames_kernel,
        (l_shape, l_shape, r_shape, r_shape, g_shape, g_shape, shape((8, LANES), F32)),
        row_offset, col_offset, counts, own, r_mine, r_other, x_mine, x_other, d_mine, d_other,
        probe, amplitudes, plus, minus,
        smem=3,
        scratch=[
            pltpu.VMEM((2, tile_rows + halo, tile_cols + frame), BF16),
            pltpu.VMEM((2, frame, frame), F32),
            pltpu.VMEM((2 * frame, frame), BF16),
            pltpu.VMEM((frame, 2 * frame), BF16),
            pltpu.VMEM((frame, 2 * frame), F32),
            pltpu.VMEM((2, tile_rows + halo, tile_cols + frame), F32),
            pltpu.VMEM((3, frame, frame), F32),
        ],
        flops=4 * 32 * frame**3,
        name="frames",
    )
    rrecv = swapped(rsend, "mode", 1)
    grecv = swapped(gsend, "mode", 1)
    rrecv, grecv, lsend = lax.optimization_barrier((rrecv, grecv, lsend))
    lrecv = swapped(lsend, "mode", 1)

    quarter = frame // 2
    g_out = (shape((2, quarter, frame), F32), shape((2 * quarter + PAD, frame), I16))
    w_out = (shape((quarter, frame), F32), shape((quarter + PAD, frame), I16))
    all_out = (shape((3, quarter, frame), F32), shape((3 * quarter + PAD, frame), I16))
    row_steps = [("row", 1 << k) for k in range(rows_count.bit_length() - 1)]
    col_steps = [("col", 1 << k) for k in range(cols_count.bit_length() - 1)]

    xsend, g, gcode, w, wcode = vmem_call(
        after_mode_kernel, (shape((held * 3 + PAD, LANES), I16), *g_out, *w_out),
        rkeep, rrecv, gkeep, grecv, name="after_mode",
    )
    xrecv = moved_along(xsend, "col", 1)
    gother, wother = swapped(gcode, *row_steps[0]), swapped(wcode, *row_steps[1])
    sums, code = vmem_call(joined_kernel, all_out, g, gother, w, wother, name="joined")
    xrecv, code = lax.optimization_barrier((xrecv, code))
    came = swapped(code, *col_steps[0])
    tile, rowsend = vmem_call(
        from_left_kernel,
        (shape((2, mid, tile_cols), F32), shape((2 * part + PAD, tile_cols), I16)),
        lkeep, lrecv, xrecv, name="from_left",
    )
    rowrecv = moved_along(rowsend, "row", 1)
    for step in row_steps[2:] + col_steps[1:]:
        sums, code = vmem_call(again_kernel, all_out, sums, came, name="again")
        came = swapped(code, *step)
    g, gcode, w, wcode = vmem_call(split_kernel, (*g_out, *w_out), sums, came, name="split")
    gother, wother = swapped(gcode, *row_steps[1]), swapped(wcode, *row_steps[0])

    rowrecv, w = lax.optimization_barrier((rowrecv, w))
    rows, spill = vmem_call(
        from_above_kernel,
        (shape((2, part, tile_cols), F32), shape((2, mid - part, tile_cols), F32)), rowrecv, name="from_above",
    )
    spilled = swapped(spill, "mode", 1)
    (object_new,) = vmem_call(
        object_kernel, (shape((mid, 2, tile_cols), F32),), object_field, tile, rows, spilled, peak, name="object"
    )
    object_new, gother = lax.optimization_barrier((object_new, gother))
    (step,) = vmem_call(probe_kernel, (shape((2, quarter, frame), F32),), g, gother, w, wother, name="probe")
    other = swapped(step, "mode", 1)
    (probe_new,) = vmem_call(
        probe_out_kernel, (shape(probe_field.shape, F32),), probe_field, step, other, name="probe_out"
    )
    return (object_new, probe_new)


def solution(mesh):
    placed = (
        P(("groups", "row"), None, "col"),
        P("groups", None, None),
        P(("groups", "row", "col", "mode"), None, None),
        P(("groups", "row", "col", "mode")),
        P(("groups", "row", "col", "mode")),
        P(("groups", "row", "col", "mode")),
    )
    return jax.shard_map(
        body,
        mesh=mesh,
        in_specs=placed,
        out_specs=(P(("groups", "row", "mode"), None, "col"), P("groups", None, None)),
        check_vma=False,
    )
```

```python
import math

import jax
import jax.numpy as jnp
import numpy as np
from jax import lax
from jax.experimental import pallas as pl
from jax.experimental.pallas import tpu as pltpu
from jax.sharding import PartitionSpec as P

MODULUS_FLOOR = 0.5
EPSILON = 1e-05
REGULARIZER = 1.0
STEP = 64
LANES = 128
PAD = 16
BITS = 14
CHUNK = 32
GROUP = 2
STAGGER = 2

F32 = jnp.float32
BF16 = jnp.bfloat16
I16 = jnp.int16


def dft_tables(points):
    index = np.arange(points)
    product = (index[:, None] * index[None, :]) % points
    angle = np.float32(2.0 * math.pi / points) * product.astype(np.float32)
    norm = 1.0 / math.sqrt(points)
    cosine = (np.cos(angle) * np.float32(norm)).astype(np.float32)
    sine = (np.sin(angle) * np.float32(norm)).astype(np.float32)
    plus = np.block([[cosine, sine], [-sine, cosine]])
    minus = np.block([[cosine, -sine], [sine, cosine]])
    return jnp.asarray(plus, BF16), jnp.asarray(minus, BF16)


def vmem_call(kernel, outs, *operands, smem=0, scratch=(), flops=0, name=None):
    specs = [pl.BlockSpec(memory_space=pltpu.SMEM)] * smem
    specs += [pl.BlockSpec(memory_space=pltpu.VMEM)] * (len(operands) - smem)
    moved = sum(math.prod(o.shape) * o.dtype.itemsize for o in (*operands, *outs))
    return pl.pallas_call(
        kernel,
        out_shape=tuple(jax.ShapeDtypeStruct(o.shape, o.dtype) for o in outs),
        in_specs=specs,
        out_specs=tuple(pl.BlockSpec(memory_space=pltpu.VMEM) for _ in outs),
        scratch_shapes=scratch,
        compiler_params=pltpu.CompilerParams(vmem_limit_bytes=40 * 1024 * 1024),
        cost_estimate=pl.CostEstimate(flops=flops, bytes_accessed=moved, transcendentals=0),
        name=name,
    )(*operands)


def shape(dims, dtype):
    return jax.ShapeDtypeStruct(dims, dtype)


def encode(block):
    peak = jnp.max(jnp.abs(block), axis=0, keepdims=True)
    power = jnp.ceil(jnp.log2(jnp.maximum(peak, 1e-30)))
    whole = jnp.round(block * jnp.exp2(BITS - power))
    return whole.astype(jnp.int32).astype(I16), power, whole * jnp.exp2(power - BITS)


def encode_to(ref, blocks):
    rows, cols = blocks[0].shape
    tail = jnp.zeros((PAD, cols), F32)
    row = lax.broadcasted_iota(jnp.int32, (PAD, cols), 0)
    decoded = []
    for n, block in enumerate(blocks):
        code, power, back = encode(block)
        ref[n * rows : (n + 1) * rows, :] = code
        tail = jnp.where(row == n, power, tail)
        decoded.append(back)
    ref[len(blocks) * rows :, :] = tail.astype(jnp.int32).astype(I16)
    return decoded


def decode(ref, count):
    rows = (ref.shape[0] - PAD) // count
    tail = ref[count * rows :, :].astype(jnp.int32).astype(F32)
    return [
        ref[n * rows : (n + 1) * rows, :].astype(jnp.int32).astype(F32) * jnp.exp2(tail[n : n + 1] - BITS)
        for n in range(count)
    ]


def turned(value):
    return pltpu.roll(value, STEP, 1)


def low_lanes(rows):
    return lax.broadcasted_iota(jnp.int32, (rows, LANES), 1) < STEP


def folded(first, second):
    mid = first.shape[0] // 2
    return jnp.concatenate([first, jnp.where(low_lanes(mid), second[:mid], turned(second[mid:]))], axis=0)


def unfolded(block):
    rows = block.shape[0] * 2 // 3
    tail, low = block[rows:], low_lanes(rows // 2)
    zero = jnp.zeros_like(tail)
    second = jnp.concatenate([jnp.where(low, tail, zero), jnp.where(low, turned(tail), zero)], axis=0)
    return jnp.concatenate([block[:rows], second], axis=1)


def frames_kernel(
    row_ref, col_ref, count_ref, own_ref, r_mine, r_other, x_mine, x_other, d_mine, d_other,
    probe_ref, amp_ref, plus_ref, minus_ref,
    lkeep_ref, lsend_ref, rkeep_ref, rsend_ref, gkeep_ref, gsend_ref, peak_ref,
    ext, patch, wave, half, field, total, grads,
):
    _, tile_rows, tile_cols = own_ref.shape
    frame = probe_ref.shape[1]
    part = r_mine.shape[1]
    mid = tile_rows // 2
    mode = lax.axis_index("mode")
    top = lax.axis_index("row") * tile_rows
    left = lax.axis_index("col") * tile_cols

    ext[:, :tile_rows, :tile_cols] = own_ref[...]
    for who, below, right, diagonal in ((mode, r_mine, x_mine, d_mine), (1 - mode, r_other, x_other, d_other)):
        rows = pl.ds(pl.multiple_of(tile_rows + who * part, 32), part)
        ext[:, rows, :tile_cols] = below[...]
        ext[:, rows, tile_cols:] = diagonal[...]
        ext[:, pl.ds(pl.multiple_of(who * mid, mid), mid), tile_cols:] = right[...]

    power = probe_ref[0] * probe_ref[0] + probe_ref[1] * probe_ref[1]
    peak_ref[...] = jnp.broadcast_to(jnp.max(power, keepdims=True), peak_ref.shape) + EPSILON

    total[...] = jnp.zeros(total.shape, F32)
    grads[...] = jnp.zeros(grads.shape, F32)
    tiles = frame // LANES
    low = low_lanes(CHUNK)

    count = amp_ref.shape[0]
    base_row = [pl.multiple_of(row_ref[n] - top, STEP) for n in range(count)]
    shift = [col_ref[n] - left for n in range(count)]
    odd = [(shift[n] // STEP) % 2 == 1 for n in range(count)]
    base_col = [pl.multiple_of((shift[n] // LANES) * LANES, LANES) for n in range(count)]
    live = [jnp.where(n < count_ref[0], 1.0, 0.0) for n in range(count)]

    def window(n, plane, start):
        rows = pl.ds(pl.multiple_of(base_row[n] + start, CHUNK), CHUNK)
        return plane, rows, pl.ds(base_col[n], frame + LANES)

    def tile_of(value, t):
        return value[:, t * LANES : (t + 1) * LANES]

    def exit_wave(n):
        for start in range(0, frame, CHUNK):
            rows = pl.ds(start, CHUNK)
            obj = []
            for plane in range(2):
                got = ext[window(n, plane, start)].astype(F32)
                pieces = [tile_of(got, t) for t in range(tiles + 1)]
                rolled = [turned(piece) for piece in pieces]
                chosen = [
                    jnp.where(odd[n], jnp.where(low, rolled[t], rolled[t + 1]), pieces[t]) for t in range(tiles)
                ]
                obj.append(jnp.concatenate(chosen, axis=1))
                patch[n, plane, rows, :] = obj[plane].astype(BF16)
            p_re, p_im = probe_ref[0, rows, :], probe_ref[1, rows, :]
            wave[n, rows, :] = (p_re * obj[0] - p_im * obj[1]).astype(BF16)
            wave[n, pl.ds(frame + start, CHUNK), :] = (p_re * obj[1] + p_im * obj[0]).astype(BF16)

    def left_product(n, table):
        first = jnp.dot(table[...], wave[n], preferred_element_type=F32)
        half[n, :, :frame] = first[:frame].astype(BF16)
        half[n, :, frame:] = first[frame:].astype(BF16)

    def right_product(n, table):
        field[n] = jnp.dot(half[n], table[...], preferred_element_type=F32)

    def change(n):
        for start in range(0, frame, CHUNK):
            rows = pl.ds(start, CHUNK)
            re, im = field[n, rows, :frame], field[n, rows, frame:]
            inverse = jnp.minimum(lax.rsqrt(re * re + im * im), 1.0 / MODULUS_FLOOR)
            factor = (amp_ref[n, rows, :].astype(F32) * inverse - 1.0) * live[n]
            wave[n, rows, :] = (re * factor).astype(BF16)
            wave[n, pl.ds(frame + start, CHUNK), :] = (im * factor).astype(BF16)

    def update(n):
        for start in range(0, frame, CHUNK):
            rows = pl.ds(start, CHUNK)
            re, im = field[n, rows, :frame], field[n, rows, frame:]
            p_re, p_im = probe_ref[0, rows, :], probe_ref[1, rows, :]
            o_re, o_im = patch[n, 0, rows, :].astype(F32), patch[n, 1, rows, :].astype(F32)
            steps = (p_re * re + p_im * im, p_re * im - p_im * re)
            for plane in range(2):
                pieces = [tile_of(steps[plane], t) for t in range(tiles)]
                rolled = [turned(piece) for piece in pieces]
                zero = jnp.zeros_like(pieces[0])
                moved = []
                for t in range(tiles + 1):
                    before = rolled[t - 1] if t > 0 else zero
                    here = rolled[t] if t < tiles else zero
                    moved.append(
                        jnp.where(odd[n], jnp.where(low, before, here), pieces[t] if t < tiles else zero)
                    )
                total[window(n, plane, start)] += jnp.concatenate(moved, axis=1)
            grads[0, rows, :] += o_re * re + o_im * im
            grads[1, rows, :] += o_re * im - o_im * re
            grads[2, rows, :] += (o_re * o_re + o_im * o_im) * live[n]

    stages = (
        exit_wave,
        lambda n: left_product(n, plus_ref),
        lambda n: right_product(n, minus_ref),
        change,
        lambda n: left_product(n, minus_ref),
        lambda n: right_product(n, plus_ref),
        update,
    )
    groups = [range(n, min(n + GROUP, count)) for n in range(0, count, GROUP)]
    for time in range(len(stages) + STAGGER * (len(groups) - 1)):
        for place in reversed(range(len(groups))):
            if 0 <= time - STAGGER * place < len(stages):
                for n in groups[place]:
                    stages[time - STAGGER * place](n)

    part_frame = frame // 2
    for who, l_ref, r_ref, g_ref in ((1 - mode, lsend_ref, rsend_ref, gsend_ref), (mode, lkeep_ref, rkeep_ref, gkeep_ref)):
        upper = pl.ds(pl.multiple_of(who * mid, mid), mid)
        lower = pl.ds(pl.multiple_of(tile_rows + who * part, 32), part)
        l_ref[:, :mid, :] = total[:, upper, :tile_cols]
        l_ref[:, mid:, :] = total[:, lower, :tile_cols]
        for plane in range(2):
            right = jnp.concatenate([total[plane, upper, tile_cols:], total[plane, lower, tile_cols:]], axis=0)
            r_ref[plane] = folded(right[:, :LANES], right[:, LANES:])
        g_ref[...] = grads[:, pl.ds(pl.multiple_of(who * part_frame, part_frame), part_frame), :]


def after_mode_kernel(rkeep, rrecv, gkeep, grecv, xsend_ref, g_ref, gsend_ref, w_ref, wsend_ref):
    encode_to(xsend_ref, [rkeep[plane] + rrecv[plane] for plane in range(2)])
    sums = [gkeep[plane] + grecv[plane] for plane in range(3)]
    g_ref[0], g_ref[1] = encode_to(gsend_ref, sums[:2])
    (w_ref[...],) = encode_to(wsend_ref, sums[2:])


def joined_kernel(g, grecv, w, wrecv, sums_ref, send_ref):
    got = decode(grecv, 2)
    sums = [g[plane] + got[plane] for plane in range(2)] + [w[...] + decode(wrecv, 1)[0]]
    sums_ref[0], sums_ref[1], sums_ref[2] = encode_to(send_ref, sums)


def split_kernel(sums, recv, g_ref, gsend_ref, w_ref, wsend_ref):
    total = [sums[plane] + got for plane, got in enumerate(decode(recv, 3))]
    g_ref[0], g_ref[1] = encode_to(gsend_ref, total[:2])
    (w_ref[...],) = encode_to(wsend_ref, total[2:])


def again_kernel(sums, recv, sums_ref, send_ref):
    total = [sums[plane] + got for plane, got in enumerate(decode(recv, 3))]
    sums_ref[0], sums_ref[1], sums_ref[2] = encode_to(send_ref, total)


def from_left_kernel(lkeep, lrecv, xrecv, tile_ref, rowsend_ref):
    rows = tile_ref.shape[1]
    came = jnp.where(lax.axis_index("col") > 0, 1.0, 0.0)
    below = []
    for plane, code in enumerate(decode(xrecv, 2)):
        got = unfolded(code) * came
        frame = got.shape[1]
        tile_ref[plane, :, :frame] = lkeep[plane, :rows, :frame] + lrecv[plane, :rows, :frame] + got[:rows]
        tile_ref[plane, :, frame:] = lkeep[plane, :rows, frame:] + lrecv[plane, :rows, frame:]
        near = lkeep[plane, rows:, :frame] + lrecv[plane, rows:, :frame] + got[rows:]
        far = lkeep[plane, rows:, frame:] + lrecv[plane, rows:, frame:]
        below.append(jnp.concatenate([near, far], axis=1))
    encode_to(rowsend_ref, below)


def from_above_kernel(rowrecv, rows_ref, spill_ref):
    got = decode(rowrecv, 2)
    came = jnp.where(lax.axis_index("row") > 0, 1.0, 0.0)
    over = spill_ref.shape[1]
    for plane in range(2):
        rows_ref[plane] = got[plane] * came
        spill_ref[plane] = got[plane][:over] * came


def object_kernel(object_ref, tile, rows, spilled, peak, out_ref):
    mode = lax.axis_index("mode")
    mid, part = tile.shape[1], rows.shape[1]
    over = mid - part
    scale = 1.0 / peak[0:1, 0:1]
    for who in range(2):

        @pl.when(mode == who)
        def _(who=who):
            for plane in range(2):
                for start in range(0, mid, CHUNK):
                    step = tile[plane, start : start + CHUNK, :]
                    if who == 0:
                        step += rows[plane, start : start + CHUNK, :] if start < part else spilled[plane, start - part :, :]
                    elif start < part - over:
                        step += rows[plane, start + over : start + over + CHUNK, :]
                    old = object_ref[who * mid + start : who * mid + start + CHUNK, plane, :]
                    out_ref[start : start + CHUNK, plane, :] = old + step * scale


def probe_kernel(g, grecv, w, wrecv, step_ref):
    weight = w[...] + decode(wrecv, 1)[0] + REGULARIZER
    got = decode(grecv, 2)
    for plane in range(2):
        step_ref[plane] = (g[plane] + got[plane]) / weight


def probe_out_kernel(probe_ref, mine, other, out_ref):
    mode = lax.axis_index("mode")
    rows = mine.shape[1]
    for start in range(0, rows, CHUNK):
        for plane in range(2):
            one, two = mine[plane, start : start + CHUNK, :], other[plane, start : start + CHUNK, :]
            first, second = jnp.where(mode == 0, one, two), jnp.where(mode == 0, two, one)
            for place, step in ((start, first), (rows + start, second)):
                old = probe_ref[place : place + CHUNK, plane, :]
                out_ref[place : place + CHUNK, plane, :] = old + step


def moved_along(value, axis, steps):
    count = lax.axis_size(axis)
    if count == 2:
        return swapped(value, axis, 1)
    first, last = (max(0, -steps), min(count, count - steps))
    return lax.ppermute(value, axis, [(source, source + steps) for source in range(first, last)])


def swapped(value, axis, distance):
    count = lax.axis_size(axis)
    return lax.ppermute(value, axis, [(source, source ^ distance) for source in range(count)])


def frames(row_offset, col_offset, counts, own, pieces, probe, amplitudes, plus, minus):
    _, tile_rows, tile_cols = own.shape
    frame = probe.shape[1]
    halo = frame - STEP
    held = (tile_rows + halo) // 2
    count = amplitudes.shape[0]
    l_shape = shape((2, held, tile_cols), F32)
    r_shape = shape((2, held * 3 // 2, LANES), F32)
    g_shape = shape((3, frame // 2, frame), F32)
    return vmem_call(
        frames_kernel,
        (l_shape, l_shape, r_shape, r_shape, g_shape, g_shape, shape((8, LANES), F32)),
        row_offset, col_offset, counts, own, *pieces, probe, amplitudes, plus, minus,
        smem=3,
        scratch=[
            pltpu.VMEM((2, tile_rows + halo, tile_cols + frame), BF16),
            pltpu.VMEM((count, 2, frame, frame), BF16),
            pltpu.VMEM((count, 2 * frame, frame), BF16),
            pltpu.VMEM((count, frame, 2 * frame), BF16),
            pltpu.VMEM((count, frame, 2 * frame), F32),
            pltpu.VMEM((2, tile_rows + halo, tile_cols + frame), F32),
            pltpu.VMEM((3, frame, frame), F32),
        ],
        flops=4 * 32 * frame**3,
        name="frames",
    )


def body(object_field, probe_field, amplitudes, row_offset, col_offset, counts):
    tile_rows, _, tile_cols = object_field.shape
    frame = probe_field.shape[0]
    halo = frame - STEP
    part, mid = halo // 2, tile_rows // 2
    rows_count, cols_count = lax.axis_size("row"), lax.axis_size("col")
    mode = lax.axis_index("mode")
    plus, minus = dft_tables(frame)

    def planar(block):
        return jnp.transpose(block.astype(BF16), (1, 0, 2))

    r_send = planar(lax.dynamic_slice_in_dim(object_field, mode * part, part, 0))
    x_send = planar(lax.dynamic_slice_in_dim(object_field[:, :, :frame], mode * mid, mid, 0))
    r_send, x_send = lax.optimization_barrier((r_send, x_send))
    d_send = r_send[:, :, :frame]
    diagonal = []
    for r in range(1, rows_count):
        for c in range(1, cols_count):
            here = r * cols_count + c
            diagonal.append((here, here - cols_count - 1))
    r_mine = moved_along(r_send, "row", -1)
    d_mine = lax.ppermute(d_send, ("row", "col"), diagonal)
    x_mine = moved_along(x_send, "col", -1)
    r_mine, d_mine, x_mine = lax.optimization_barrier((r_mine, d_mine, x_mine))
    r_other, d_other, x_other = (swapped(v, "mode", 1) for v in (r_mine, d_mine, x_mine))
    own = planar(object_field)
    probe = jnp.transpose(probe_field, (1, 0, 2))

    pieces = (r_mine, r_other, x_mine, x_other, d_mine, d_other)
    lkeep, lsend, rkeep, rsend, gkeep, gsend, peak = frames(
        row_offset, col_offset, counts, own, pieces, probe, amplitudes, plus, minus
    )
    held = mid + part
    rrecv = swapped(rsend, "mode", 1)
    grecv = swapped(gsend, "mode", 1)
    rrecv, grecv, lsend = lax.optimization_barrier((rrecv, grecv, lsend))
    lrecv = swapped(lsend, "mode", 1)

    quarter = frame // 2
    g_out = (shape((2, quarter, frame), F32), shape((2 * quarter + PAD, frame), I16))
    w_out = (shape((quarter, frame), F32), shape((quarter + PAD, frame), I16))
    all_out = (shape((3, quarter, frame), F32), shape((3 * quarter + PAD, frame), I16))
    row_steps = [("row", 1 << k) for k in range(rows_count.bit_length() - 1)]
    col_steps = [("col", 1 << k) for k in range(cols_count.bit_length() - 1)]

    xsend, g, gcode, w, wcode = vmem_call(
        after_mode_kernel, (shape((held * 3 + PAD, LANES), I16), *g_out, *w_out),
        rkeep, rrecv, gkeep, grecv, name="after_mode",
    )
    xrecv = moved_along(xsend, "col", 1)
    gother, wother = swapped(gcode, *row_steps[0]), swapped(wcode, *row_steps[1])
    sums, code = vmem_call(joined_kernel, all_out, g, gother, w, wother, name="joined")
    xrecv, code = lax.optimization_barrier((xrecv, code))
    came = swapped(code, *col_steps[0])
    tile, rowsend = vmem_call(
        from_left_kernel,
        (shape((2, mid, tile_cols), F32), shape((2 * part + PAD, tile_cols), I16)),
        lkeep, lrecv, xrecv, name="from_left",
    )
    rowrecv = moved_along(rowsend, "row", 1)
    for step in row_steps[2:] + col_steps[1:]:
        sums, code = vmem_call(again_kernel, all_out, sums, came, name="again")
        came = swapped(code, *step)
    g, gcode, w, wcode = vmem_call(split_kernel, (*g_out, *w_out), sums, came, name="split")
    gother, wother = swapped(gcode, *row_steps[1]), swapped(wcode, *row_steps[0])

    rowrecv, w = lax.optimization_barrier((rowrecv, w))
    rows, spill = vmem_call(
        from_above_kernel,
        (shape((2, part, tile_cols), F32), shape((2, mid - part, tile_cols), F32)), rowrecv, name="from_above",
    )
    spilled = swapped(spill, "mode", 1)
    (object_new,) = vmem_call(
        object_kernel, (shape((mid, 2, tile_cols), F32),), object_field, tile, rows, spilled, peak, name="object"
    )
    object_new, gother = lax.optimization_barrier((object_new, gother))
    (step,) = vmem_call(probe_kernel, (shape((2, quarter, frame), F32),), g, gother, w, wother, name="probe")
    other = swapped(step, "mode", 1)
    (probe_new,) = vmem_call(
        probe_out_kernel, (shape(probe_field.shape, F32),), probe_field, step, other, name="probe_out"
    )
    return (object_new, probe_new)


def solution(mesh):
    placed = (
        P(("groups", "row"), None, "col"),
        P("groups", None, None),
        P(("groups", "row", "col", "mode"), None, None),
        P(("groups", "row", "col", "mode")),
        P(("groups", "row", "col", "mode")),
        P(("groups", "row", "col", "mode")),
    )
    return jax.shard_map(
        body,
        mesh=mesh,
        in_specs=placed,
        out_specs=(P(("groups", "row", "mode"), None, "col"), P("groups", None, None)),
        check_vma=False,
    )
```

```python
import math

import jax
import jax.numpy as jnp
import numpy as np
from jax import lax
from jax.experimental import pallas as pl
from jax.experimental.pallas import tpu as pltpu
from jax.sharding import PartitionSpec as P

MODULUS_FLOOR = 0.5
EPSILON = 1e-05
REGULARIZER = 1.0
STEP = 64
LANES = 128
PAD = 16
WTAIL = 272
BITS = 14
CHUNK = 32
GROUP = 2
STAGGER = 2

F32 = jnp.float32
BF16 = jnp.bfloat16
I16 = jnp.int16


def dft_tables(points):
    index = np.arange(points)
    product = (index[:, None] * index[None, :]) % points
    angle = np.float32(2.0 * math.pi / points) * product.astype(np.float32)
    norm = 1.0 / math.sqrt(points)
    cosine = (np.cos(angle) * np.float32(norm)).astype(np.float32)
    sine = (np.sin(angle) * np.float32(norm)).astype(np.float32)
    plus = np.block([[cosine, sine], [-sine, cosine]])
    minus = np.block([[cosine, -sine], [sine, cosine]])
    return jnp.asarray(plus, BF16), jnp.asarray(minus, BF16)


def vmem_call(kernel, outs, *operands, smem=0, far=(), far_out=False, into=None, scratch=(), flops=0, name=None):
    places = [pltpu.SMEM if n < smem else pltpu.HBM if n in far else pltpu.VMEM for n in range(len(operands))]
    moved = sum(math.prod(o.shape) * o.dtype.itemsize for o in (*operands, *outs))
    return pl.pallas_call(
        kernel,
        out_shape=tuple(jax.ShapeDtypeStruct(o.shape, o.dtype) for o in outs),
        in_specs=[pl.BlockSpec(memory_space=place) for place in places],
        out_specs=tuple(pl.BlockSpec(memory_space=pltpu.HBM if far_out else pltpu.VMEM) for _ in outs),
        scratch_shapes=scratch,
        input_output_aliases={} if into is None else {into: 0},
        compiler_params=pltpu.CompilerParams(vmem_limit_bytes=40 * 1024 * 1024),
        cost_estimate=pl.CostEstimate(flops=flops, bytes_accessed=moved, transcendentals=0),
        name=name,
    )(*operands)


def shape(dims, dtype):
    return jax.ShapeDtypeStruct(dims, dtype)


def encode(block):
    peak = jnp.max(jnp.abs(block), axis=0, keepdims=True)
    power = jnp.ceil(jnp.log2(jnp.maximum(peak, 1e-30)))
    whole = jnp.round(block * jnp.exp2(BITS - power))
    return whole.astype(jnp.int32).astype(I16), power, whole * jnp.exp2(power - BITS)


def tile_of(value, tile):
    return value[:, tile * LANES : (tile + 1) * LANES]


def code_shape(planes, rows, cols, tail=PAD):
    return shape((planes * rows * cols // LANES + tail, LANES), I16)


def encode_to(ref, planes):
    rows, cols = planes[0].shape
    tail = jnp.zeros((PAD, LANES), F32)
    row = lax.broadcasted_iota(jnp.int32, (PAD, LANES), 0)
    decoded, n = [], 0
    for plane in planes:
        blocks = []
        for tile in range(cols // LANES):
            code, power, back = encode(tile_of(plane, tile))
            ref[n * rows : (n + 1) * rows, :] = code
            tail = jnp.where(row == n, power, tail)
            blocks.append(back)
            n += 1
        decoded.append(jnp.concatenate(blocks, axis=1))
    ref[n * rows : n * rows + PAD, :] = tail.astype(jnp.int32).astype(I16)
    if ref.shape[0] > n * rows + PAD:
        ref[n * rows + PAD :, :] = jnp.zeros((ref.shape[0] - n * rows - PAD, LANES), I16)
    return decoded


def decode(ref, planes, rows, cols):
    tiles = cols // LANES
    first = planes * tiles * rows
    tail = ref[first : first + PAD, :].astype(jnp.int32).astype(F32)
    blocks = [
        ref[n * rows : (n + 1) * rows, :].astype(jnp.int32).astype(F32) * jnp.exp2(tail[n : n + 1] - BITS)
        for n in range(planes * tiles)
    ]
    return [jnp.concatenate(blocks[n * tiles : (n + 1) * tiles], axis=1) for n in range(planes)]


def turned(value):
    return pltpu.roll(value, STEP, 1)


def low_lanes(rows):
    return lax.broadcasted_iota(jnp.int32, (rows, LANES), 1) < STEP


def folded(first, second):
    mid = first.shape[0] // 2
    return jnp.concatenate([first, jnp.where(low_lanes(mid), second[:mid], turned(second[mid:]))], axis=0)


def unfolded(block):
    rows = block.shape[0] * 2 // 3
    tail, low = block[rows:], low_lanes(rows // 2)
    zero = jnp.zeros_like(tail)
    second = jnp.concatenate([jnp.where(low, tail, zero), jnp.where(low, turned(tail), zero)], axis=0)
    return jnp.concatenate([block[:rows], second], axis=1)


def frames_kernel(
    row_ref, col_ref, count_ref, own_ref, r_mine, r_other, x_mine, x_other, d_mine, d_other,
    probe_ref, amp_ref, plus_ref, minus_ref,
    lkeep_ref, lsend_ref, rkeep_ref, rsend_ref, gkeep_ref, gsend_ref, peak_ref,
    ext, patch, wave, half, field, total, grads,
):
    _, tile_rows, tile_cols = own_ref.shape
    frame = probe_ref.shape[1]
    part = r_mine.shape[1]
    mid = tile_rows // 2
    mode = lax.axis_index("mode")
    top = lax.axis_index("row") * tile_rows
    left = lax.axis_index("col") * tile_cols

    ext[:, :tile_rows, :tile_cols] = own_ref[...]
    for who, below, right, diagonal in ((mode, r_mine, x_mine, d_mine), (1 - mode, r_other, x_other, d_other)):
        rows = pl.ds(pl.multiple_of(tile_rows + who * part, 32), part)
        ext[:, rows, :tile_cols] = below[...]
        for plane in range(2):
            ext[plane, rows, tile_cols:] = unfolded(diagonal[plane].astype(F32)).astype(BF16)
        ext[:, pl.ds(pl.multiple_of(who * mid, mid), mid), tile_cols : tile_cols + right.shape[2]] = right[...]

    power = probe_ref[0] * probe_ref[0] + probe_ref[1] * probe_ref[1]
    peak_ref[...] = jnp.broadcast_to(jnp.max(power, keepdims=True), peak_ref.shape) + EPSILON

    total[...] = jnp.zeros(total.shape, F32)
    grads[...] = jnp.zeros(grads.shape, F32)
    tiles = frame // LANES
    low = low_lanes(CHUNK)

    count = amp_ref.shape[0]
    base_row = [pl.multiple_of(row_ref[n] - top, STEP) for n in range(count)]
    shift = [col_ref[n] - left for n in range(count)]
    odd = [(shift[n] // STEP) % 2 == 1 for n in range(count)]
    base_col = [pl.multiple_of((shift[n] // LANES) * LANES, LANES) for n in range(count)]
    live = [jnp.where(n < count_ref[0], 1.0, 0.0) for n in range(count)]

    def window(n, plane, start):
        rows = pl.ds(pl.multiple_of(base_row[n] + start, CHUNK), CHUNK)
        return plane, rows, pl.ds(base_col[n], frame + LANES)

    def exit_wave(n):
        for start in range(0, frame, CHUNK):
            rows = pl.ds(start, CHUNK)
            obj = []
            for plane in range(2):
                got = ext[window(n, plane, start)].astype(F32)
                pieces = [tile_of(got, t) for t in range(tiles + 1)]
                rolled = [turned(piece) for piece in pieces]
                chosen = [
                    jnp.where(odd[n], jnp.where(low, rolled[t], rolled[t + 1]), pieces[t]) for t in range(tiles)
                ]
                obj.append(jnp.concatenate(chosen, axis=1))
                patch[n, plane, rows, :] = obj[plane].astype(BF16)
            p_re, p_im = probe_ref[0, rows, :], probe_ref[1, rows, :]
            wave[n, rows, :] = (p_re * obj[0] - p_im * obj[1]).astype(BF16)
            wave[n, pl.ds(frame + start, CHUNK), :] = (p_re * obj[1] + p_im * obj[0]).astype(BF16)

    def left_product(n, table):
        first = jnp.dot(table[...], wave[n], preferred_element_type=F32)
        half[n, :, :frame] = first[:frame].astype(BF16)
        half[n, :, frame:] = first[frame:].astype(BF16)

    def right_product(n, table):
        field[n] = jnp.dot(half[n], table[...], preferred_element_type=F32)

    def change(n):
        for start in range(0, frame, CHUNK):
            rows = pl.ds(start, CHUNK)
            re, im = field[n, rows, :frame], field[n, rows, frame:]
            inverse = jnp.minimum(lax.rsqrt(re * re + im * im), 1.0 / MODULUS_FLOOR)
            factor = (amp_ref[n, rows, :].astype(F32) * inverse - 1.0) * live[n]
            wave[n, rows, :] = (re * factor).astype(BF16)
            wave[n, pl.ds(frame + start, CHUNK), :] = (im * factor).astype(BF16)

    def update(n):
        for start in range(0, frame, CHUNK):
            rows = pl.ds(start, CHUNK)
            re, im = field[n, rows, :frame], field[n, rows, frame:]
            p_re, p_im = probe_ref[0, rows, :], probe_ref[1, rows, :]
            o_re, o_im = patch[n, 0, rows, :].astype(F32), patch[n, 1, rows, :].astype(F32)
            steps = (p_re * re + p_im * im, p_re * im - p_im * re)
            for plane in range(2):
                pieces = [tile_of(steps[plane], t) for t in range(tiles)]
                rolled = [turned(piece) for piece in pieces]
                zero = jnp.zeros_like(pieces[0])
                moved = []
                for t in range(tiles + 1):
                    before = rolled[t - 1] if t > 0 else zero
                    here = rolled[t] if t < tiles else zero
                    moved.append(
                        jnp.where(odd[n], jnp.where(low, before, here), pieces[t] if t < tiles else zero)
                    )
                total[window(n, plane, start)] += jnp.concatenate(moved, axis=1)
            grads[0, rows, :] += o_re * re + o_im * im
            grads[1, rows, :] += o_re * im - o_im * re
            grads[2, rows, :] += (o_re * o_re + o_im * o_im) * live[n]

    stages = (
        exit_wave,
        lambda n: left_product(n, plus_ref),
        lambda n: right_product(n, minus_ref),
        change,
        lambda n: left_product(n, minus_ref),
        lambda n: right_product(n, plus_ref),
        update,
    )
    groups = [range(n, min(n + GROUP, count)) for n in range(0, count, GROUP)]
    for time in range(len(stages) + STAGGER * (len(groups) - 1)):
        for place in reversed(range(len(groups))):
            if 0 <= time - STAGGER * place < len(stages):
                for n in groups[place]:
                    stages[time - STAGGER * place](n)

    part_frame = frame // 2
    for who, l_ref, r_ref, g_ref in ((1 - mode, lsend_ref, rsend_ref, gsend_ref), (mode, lkeep_ref, rkeep_ref, gkeep_ref)):
        upper = pl.ds(pl.multiple_of(who * mid, mid), mid)
        lower = pl.ds(pl.multiple_of(tile_rows + who * part, 32), part)
        l_ref[:, :mid, :] = total[:, upper, :tile_cols]
        l_ref[:, mid:, :] = total[:, lower, :tile_cols]
        for plane in range(2):
            right = jnp.concatenate([total[plane, upper, tile_cols:], total[plane, lower, tile_cols:]], axis=0)
            r_ref[plane] = folded(right[:, :LANES], right[:, LANES:])
        g_ref[...] = grads[:, pl.ds(pl.multiple_of(who * part_frame, part_frame), part_frame), :]


def after_mode_kernel(rkeep, rrecv, gkeep, grecv, xsend_ref, g_ref, gsend_ref, w_ref, wsend_ref):
    encode_to(xsend_ref, [rkeep[plane] + rrecv[plane] for plane in range(2)])
    sums = [gkeep[plane] + grecv[plane] for plane in range(3)]
    g_ref[0], g_ref[1] = encode_to(gsend_ref, sums[:2])
    (w_ref[...],) = encode_to(wsend_ref, sums[2:])


def joined_kernel(g, grecv, w, wrecv, sums_ref, send_ref):
    got = decode(grecv, 2, *w.shape) + decode(wrecv, 1, *w.shape)
    sums = [g[0] + got[0], g[1] + got[1], w[...] + got[2]]
    sums_ref[0], sums_ref[1], sums_ref[2] = encode_to(send_ref, sums)


def split_kernel(sums, recv, g_ref, gsend_ref, w_ref, wsend_ref):
    total = [sums[plane] + got for plane, got in enumerate(decode(recv, 3, *sums.shape[1:]))]
    g_ref[0], g_ref[1] = encode_to(gsend_ref, total[:2])
    (w_ref[...],) = encode_to(wsend_ref, total[2:])


def again_kernel(sums, recv, sums_ref, send_ref):
    total = [sums[plane] + got for plane, got in enumerate(decode(recv, 3, *sums.shape[1:]))]
    sums_ref[0], sums_ref[1], sums_ref[2] = encode_to(send_ref, total)


def from_left_kernel(lkeep, lrecv, xrecv, tile_ref, rowsend_ref):
    rows = tile_ref.shape[1]
    came = jnp.where(lax.axis_index("col") > 0, 1.0, 0.0)
    below = []
    for plane, code in enumerate(decode(xrecv, 2, lkeep.shape[1] * 3 // 2, LANES)):
        got = unfolded(code) * came
        frame = got.shape[1]
        tile_ref[plane, :, :frame] = lkeep[plane, :rows, :frame] + lrecv[plane, :rows, :frame] + got[:rows]
        tile_ref[plane, :, frame:] = lkeep[plane, :rows, frame:] + lrecv[plane, :rows, frame:]
        near = lkeep[plane, rows:, :frame] + lrecv[plane, rows:, :frame] + got[rows:]
        far = lkeep[plane, rows:, frame:] + lrecv[plane, rows:, frame:]
        below.append(jnp.concatenate([near, far], axis=1))
    encode_to(rowsend_ref, below)


def from_above_kernel(rowrecv, rows_ref, spill_ref):
    got = decode(rowrecv, 2, *rows_ref.shape[1:])
    came = jnp.where(lax.axis_index("row") > 0, 1.0, 0.0)
    over = spill_ref.shape[1]
    for plane in range(2):
        rows_ref[plane] = got[plane] * came
        spill_ref[plane] = got[plane][:over] * came


def object_kernel(object_ref, tile, rows, spilled, peak, out_ref):
    mode = lax.axis_index("mode")
    mid, part = tile.shape[1], rows.shape[1]
    over = mid - part
    scale = 1.0 / peak[0:1, 0:1]
    for who in range(2):

        @pl.when(mode == who)
        def _(who=who):
            for plane in range(2):
                for start in range(0, mid, CHUNK):
                    step = tile[plane, start : start + CHUNK, :]
                    if who == 0:
                        step += rows[plane, start : start + CHUNK, :] if start < part else spilled[plane, start - part :, :]
                    elif start < part - over:
                        step += rows[plane, start + over : start + over + CHUNK, :]
                    old = object_ref[who * mid + start : who * mid + start + CHUNK, plane, :]
                    out_ref[start : start + CHUNK, plane, :] = old + step * scale


def probe_kernel(g, grecv, w, wrecv, step_ref):
    weight = w[...] + decode(wrecv, 1, *w.shape)[0] + REGULARIZER
    got = decode(grecv, 2, *w.shape)
    for plane in range(2):
        step_ref[plane] = (g[plane] + got[plane]) / weight


def put_half(who, probe_ref, step, out_ref, block, arrived):
    rows = step.shape[1]
    place = pl.ds(pl.multiple_of(who * rows, rows), rows)
    for plane in range(2):
        block[:, plane, :] = probe_ref[place, plane, :] + step[plane]
    copy = pltpu.make_async_copy(block, out_ref.at[place], arrived)
    copy.start()
    copy.wait()


def probe_mine_kernel(probe_ref, step, out_ref, block, arrived):
    put_half(lax.axis_index("mode"), probe_ref, step, out_ref, block, arrived)


def probe_other_kernel(probe_ref, step, before_ref, out_ref, block, arrived):
    del before_ref
    put_half(1 - lax.axis_index("mode"), probe_ref, step, out_ref, block, arrived)


def moved_along(value, axis, steps):
    count = lax.axis_size(axis)
    if count == 2:
        return swapped(value, axis, 1)
    first, last = (max(0, -steps), min(count, count - steps))
    return lax.ppermute(value, axis, [(source, source + steps) for source in range(first, last)])


def swapped(value, axis, distance):
    count = lax.axis_size(axis)
    return lax.ppermute(value, axis, [(source, source ^ distance) for source in range(count)])


def frames(row_offset, col_offset, counts, own, pieces, probe, amplitudes, plus, minus):
    _, tile_rows, tile_cols = own.shape
    frame = probe.shape[1]
    halo = frame - STEP
    held = (tile_rows + halo) // 2
    count = amplitudes.shape[0]
    l_shape = shape((2, held, tile_cols), F32)
    r_shape = shape((2, held * 3 // 2, LANES), F32)
    g_shape = shape((3, frame // 2, frame), F32)
    return vmem_call(
        frames_kernel,
        (l_shape, l_shape, r_shape, r_shape, g_shape, g_shape, shape((8, LANES), F32)),
        row_offset, col_offset, counts, own, *pieces, probe, amplitudes, plus, minus,
        smem=3,
        scratch=[
            pltpu.VMEM((2, tile_rows + halo, tile_cols + frame), BF16),
            pltpu.VMEM((count, 2, frame, frame), BF16),
            pltpu.VMEM((count, 2 * frame, frame), BF16),
            pltpu.VMEM((count, frame, 2 * frame), BF16),
            pltpu.VMEM((count, frame, 2 * frame), F32),
            pltpu.VMEM((2, tile_rows + halo, tile_cols + frame), F32),
            pltpu.VMEM((3, frame, frame), F32),
        ],
        flops=4 * 32 * frame**3,
        name="frames",
    )


def body(object_field, probe_field, amplitudes, row_offset, col_offset, counts):
    tile_rows, _, tile_cols = object_field.shape
    frame = probe_field.shape[0]
    halo = frame - STEP
    part, mid = halo // 2, tile_rows // 2
    rows_count, cols_count = lax.axis_size("row"), lax.axis_size("col")
    mode = lax.axis_index("mode")
    plus, minus = dft_tables(frame)

    def planar(block):
        return jnp.transpose(block.astype(BF16), (1, 0, 2))

    r_send = planar(lax.dynamic_slice_in_dim(object_field, mode * part, part, 0))
    corner = r_send[:, :, :halo]
    thin = corner[:, :, LANES:]
    thin = jnp.concatenate([thin[:, : part // 2], thin[:, part // 2 :]], axis=2)
    d_send = jnp.concatenate([corner[:, :, :LANES], thin], axis=1)
    object_later, r_send, d_send = lax.optimization_barrier((object_field, r_send, d_send))
    x_send = planar(lax.dynamic_slice_in_dim(object_later[:, :, :halo], mode * mid, mid, 0))
    x_send, x_last = lax.optimization_barrier((x_send[:1], x_send[1:]))
    diagonal = []
    for r in range(1, rows_count):
        for c in range(1, cols_count):
            here = r * cols_count + c
            diagonal.append((here, here - cols_count - 1))
    r_mine = moved_along(r_send, "row", -1)
    d_mine = lax.ppermute(d_send, ("row", "col"), diagonal)
    x_mine, x_last = moved_along(x_send, "col", -1), moved_along(x_last, "col", -1)
    r_mine, d_mine, x_mine, x_last = lax.optimization_barrier((r_mine, d_mine, x_mine, x_last))
    x_mine = jnp.concatenate([x_mine, x_last], axis=0)
    r_other, d_other, x_other = (swapped(v, "mode", 1) for v in (r_mine, d_mine, x_mine))
    own = planar(object_later)
    probe = jnp.transpose(probe_field, (1, 0, 2))

    pieces = (r_mine, r_other, x_mine, x_other, d_mine, d_other)
    lkeep, lsend, rkeep, rsend, gkeep, gsend, peak = frames(
        row_offset, col_offset, counts, own, pieces, probe, amplitudes, plus, minus
    )
    held = mid + part
    rrecv = swapped(rsend, "mode", 1)
    grecv = swapped(gsend, "mode", 1)
    rrecv, grecv, lsend = lax.optimization_barrier((rrecv, grecv, lsend))
    lrecv = swapped(lsend, "mode", 1)

    quarter = frame // 2
    g_out = (shape((2, quarter, frame), F32), code_shape(2, quarter, frame))
    w_out = (shape((quarter, frame), F32), code_shape(1, quarter, frame))
    all_out = (shape((3, quarter, frame), F32), code_shape(3, quarter, frame))
    row_steps = [("row", 1 << k) for k in range(rows_count.bit_length() - 1)]
    col_steps = [("col", 1 << k) for k in range(cols_count.bit_length() - 1)]

    xsend, g, gcode, w, wcode = vmem_call(
        after_mode_kernel, (code_shape(2, held * 3 // 2, LANES), *g_out, *w_out),
        rkeep, rrecv, gkeep, grecv, name="after_mode",
    )
    xrecv = moved_along(xsend, "col", 1)
    gother, wother = swapped(gcode, *row_steps[0]), swapped(wcode, *row_steps[1])
    sums, code = vmem_call(joined_kernel, all_out, g, gother, w, wother, name="joined")
    xrecv, code = lax.optimization_barrier((xrecv, code))
    came = swapped(code, *col_steps[0])
    tile, rowsend = vmem_call(
        from_left_kernel,
        (shape((2, mid, tile_cols), F32), code_shape(2, part, tile_cols)),
        lkeep, lrecv, xrecv, name="from_left",
    )
    rowrecv = moved_along(rowsend, "row", 1)
    for step in row_steps[2:] + col_steps[1:]:
        sums, code = vmem_call(again_kernel, all_out, sums, came, name="again")
        came = swapped(code, *step)
    g, gcode, w, wcode = vmem_call(
        split_kernel, (*g_out, w_out[0], code_shape(1, quarter, frame, tail=WTAIL)), sums, came, name="split"
    )
    gother, wother = swapped(gcode, *row_steps[1]), swapped(wcode, *row_steps[0])

    rowrecv, w = lax.optimization_barrier((rowrecv, w))
    rows, spill = vmem_call(
        from_above_kernel,
        (shape((2, part, tile_cols), F32), shape((2, mid - part, tile_cols), F32)), rowrecv, name="from_above",
    )
    spilled = swapped(spill, "mode", 1)
    (object_new,) = vmem_call(
        object_kernel, (shape((mid, 2, tile_cols), F32),), object_field, tile, rows, spilled, peak, name="object"
    )
    object_new, gother = lax.optimization_barrier((object_new, gother))
    (step,) = vmem_call(probe_kernel, (shape((2, quarter, frame), F32),), g, gother, w, wother, name="probe")
    other = swapped(step, "mode", 1)
    out = (shape(probe_field.shape, F32),)
    scratch = [pltpu.VMEM((quarter, 2, frame), F32), pltpu.SemaphoreType.DMA]
    (half_new,) = vmem_call(
        probe_mine_kernel, out, probe_field, step, far_out=True, scratch=scratch, name="probe_mine"
    )
    (probe_new,) = vmem_call(
        probe_other_kernel, out, probe_field, other, half_new,
        far=(2,), far_out=True, into=2, scratch=scratch, name="probe_other",
    )
    return (object_new, probe_new)


def solution(mesh):
    placed = (
        P(("groups", "row"), None, "col"),
        P("groups", None, None),
        P(("groups", "row", "col", "mode"), None, None),
        P(("groups", "row", "col", "mode")),
        P(("groups", "row", "col", "mode")),
        P(("groups", "row", "col", "mode")),
    )
    return jax.shard_map(
        body,
        mesh=mesh,
        in_specs=placed,
        out_specs=(P(("groups", "row", "mode"), None, "col"), P("groups", None, None)),
        check_vma=False,
    )
```

```python
import math

import jax
import jax.numpy as jnp
import numpy as np
from jax import lax
from jax.experimental import pallas as pl
from jax.experimental.pallas import tpu as pltpu
from jax.sharding import PartitionSpec as P

MODULUS_FLOOR = 0.5
EPSILON = 1e-05
REGULARIZER = 1.0
STEP = 64
LANES = 128
PAD = 16
WTAIL = 272
BITS = 14
CHUNK = 32
GROUP = 2
STAGGER = 2

F32 = jnp.float32
BF16 = jnp.bfloat16
I16 = jnp.int16


def dft_tables(points):
    index = np.arange(points)
    product = (index[:, None] * index[None, :]) % points
    angle = np.float32(2.0 * math.pi / points) * product.astype(np.float32)
    norm = 1.0 / math.sqrt(points)
    cosine = (np.cos(angle) * np.float32(norm)).astype(np.float32)
    sine = (np.sin(angle) * np.float32(norm)).astype(np.float32)
    plus = np.block([[cosine, sine], [-sine, cosine]])
    minus = np.block([[cosine, -sine], [sine, cosine]])
    return jnp.asarray(plus, BF16), jnp.asarray(minus, BF16)


def vmem_call(kernel, outs, *operands, smem=0, far=(), far_out=False, into=None, scratch=(), flops=0, name=None):
    places = [pltpu.SMEM if n < smem else pltpu.HBM if n in far else pltpu.VMEM for n in range(len(operands))]
    moved = sum(math.prod(o.shape) * o.dtype.itemsize for o in (*operands, *outs))
    return pl.pallas_call(
        kernel,
        out_shape=tuple(jax.ShapeDtypeStruct(o.shape, o.dtype) for o in outs),
        in_specs=[pl.BlockSpec(memory_space=place) for place in places],
        out_specs=tuple(pl.BlockSpec(memory_space=pltpu.HBM if far_out else pltpu.VMEM) for _ in outs),
        scratch_shapes=scratch,
        input_output_aliases={} if into is None else {into: 0},
        compiler_params=pltpu.CompilerParams(vmem_limit_bytes=40 * 1024 * 1024),
        cost_estimate=pl.CostEstimate(flops=flops, bytes_accessed=moved, transcendentals=0),
        name=name,
    )(*operands)


def shape(dims, dtype):
    return jax.ShapeDtypeStruct(dims, dtype)


def encode(block):
    peak = jnp.max(jnp.abs(block), axis=0, keepdims=True)
    power = jnp.ceil(jnp.log2(jnp.maximum(peak, 1e-30)))
    whole = jnp.round(block * jnp.exp2(BITS - power))
    return whole.astype(jnp.int32).astype(I16), power, whole * jnp.exp2(power - BITS)


def tile_of(value, tile):
    return value[:, tile * LANES : (tile + 1) * LANES]


def code_shape(planes, rows, cols, tail=PAD):
    return shape((planes * rows * cols // LANES + tail, LANES), I16)


def encode_to(ref, planes):
    rows, cols = planes[0].shape
    tail = jnp.zeros((PAD, LANES), F32)
    row = lax.broadcasted_iota(jnp.int32, (PAD, LANES), 0)
    decoded, n = [], 0
    for plane in planes:
        blocks = []
        for tile in range(cols // LANES):
            code, power, back = encode(tile_of(plane, tile))
            ref[n * rows : (n + 1) * rows, :] = code
            tail = jnp.where(row == n, power, tail)
            blocks.append(back)
            n += 1
        decoded.append(jnp.concatenate(blocks, axis=1))
    ref[n * rows : n * rows + PAD, :] = tail.astype(jnp.int32).astype(I16)
    if ref.shape[0] > n * rows + PAD:
        ref[n * rows + PAD :, :] = jnp.zeros((ref.shape[0] - n * rows - PAD, LANES), I16)
    return decoded


def decode(ref, planes, rows, cols):
    tiles = cols // LANES
    first = planes * tiles * rows
    tail = ref[first : first + PAD, :].astype(jnp.int32).astype(F32)
    blocks = [
        ref[n * rows : (n + 1) * rows, :].astype(jnp.int32).astype(F32) * jnp.exp2(tail[n : n + 1] - BITS)
        for n in range(planes * tiles)
    ]
    return [jnp.concatenate(blocks[n * tiles : (n + 1) * tiles], axis=1) for n in range(planes)]


def turned(value):
    return pltpu.roll(value, STEP, 1)


def low_lanes(rows):
    return lax.broadcasted_iota(jnp.int32, (rows, LANES), 1) < STEP


def folded(first, second):
    mid = first.shape[0] // 2
    return jnp.concatenate([first, jnp.where(low_lanes(mid), second[:mid], turned(second[mid:]))], axis=0)


def unfolded(block):
    rows = block.shape[0] * 2 // 3
    tail, low = block[rows:], low_lanes(rows // 2)
    zero = jnp.zeros_like(tail)
    second = jnp.concatenate([jnp.where(low, tail, zero), jnp.where(low, turned(tail), zero)], axis=0)
    return jnp.concatenate([block[:rows], second], axis=1)


def frames_kernel(
    row_ref, col_ref, count_ref, own_ref, r_mine, r_other, x_mine, x_other, d_mine, d_other,
    probe_ref, amp_ref, plus_ref, minus_ref,
    lkeep_ref, lsend_ref, rkeep_ref, rsend_ref, gkeep_ref, gsend_ref,
    ext, patch, wave, half, field, total, grads,
):
    _, tile_rows, tile_cols = own_ref.shape
    frame = probe_ref.shape[1]
    part = r_mine.shape[1]
    mid = tile_rows // 2
    mode = lax.axis_index("mode")
    top = lax.axis_index("row") * tile_rows
    left = lax.axis_index("col") * tile_cols

    ext[:, :tile_rows, :tile_cols] = own_ref[...]
    for who, below, right, diagonal in ((mode, r_mine, x_mine, d_mine), (1 - mode, r_other, x_other, d_other)):
        rows = pl.ds(pl.multiple_of(tile_rows + who * part, 32), part)
        ext[:, rows, :tile_cols] = below[...]
        for plane in range(2):
            ext[plane, rows, tile_cols:] = unfolded(diagonal[plane].astype(F32)).astype(BF16)
        ext[:, pl.ds(pl.multiple_of(who * mid, mid), mid), tile_cols : tile_cols + right.shape[2]] = right[...]

    total[...] = jnp.zeros(total.shape, F32)
    grads[...] = jnp.zeros(grads.shape, F32)
    tiles = frame // LANES
    low = low_lanes(CHUNK)

    count = amp_ref.shape[0]
    base_row = [pl.multiple_of(row_ref[n] - top, STEP) for n in range(count)]
    shift = [col_ref[n] - left for n in range(count)]
    odd = [(shift[n] // STEP) % 2 == 1 for n in range(count)]
    base_col = [pl.multiple_of((shift[n] // LANES) * LANES, LANES) for n in range(count)]
    live = [jnp.where(n < count_ref[0], 1.0, 0.0) for n in range(count)]

    def window(n, plane, start):
        rows = pl.ds(pl.multiple_of(base_row[n] + start, CHUNK), CHUNK)
        return plane, rows, pl.ds(base_col[n], frame + LANES)

    def exit_wave(n):
        for start in range(0, frame, CHUNK):
            rows = pl.ds(start, CHUNK)
            obj = []
            for plane in range(2):
                got = ext[window(n, plane, start)].astype(F32)
                pieces = [tile_of(got, t) for t in range(tiles + 1)]
                rolled = [turned(piece) for piece in pieces]
                chosen = [
                    jnp.where(odd[n], jnp.where(low, rolled[t], rolled[t + 1]), pieces[t]) for t in range(tiles)
                ]
                obj.append(jnp.concatenate(chosen, axis=1))
                patch[n, plane, rows, :] = obj[plane].astype(BF16)
            p_re, p_im = probe_ref[0, rows, :], probe_ref[1, rows, :]
            wave[n, rows, :] = (p_re * obj[0] - p_im * obj[1]).astype(BF16)
            wave[n, pl.ds(frame + start, CHUNK), :] = (p_re * obj[1] + p_im * obj[0]).astype(BF16)

    def left_product(n, table):
        first = jnp.dot(table[...], wave[n], preferred_element_type=F32)
        half[n, :, :frame] = first[:frame].astype(BF16)
        half[n, :, frame:] = first[frame:].astype(BF16)

    def right_product(n, table):
        field[n] = jnp.dot(half[n], table[...], preferred_element_type=F32)

    def change(n):
        for start in range(0, frame, CHUNK):
            rows = pl.ds(start, CHUNK)
            re, im = field[n, rows, :frame], field[n, rows, frame:]
            inverse = jnp.minimum(lax.rsqrt(re * re + im * im), 1.0 / MODULUS_FLOOR)
            factor = (amp_ref[n, rows, :].astype(F32) * inverse - 1.0) * live[n]
            wave[n, rows, :] = (re * factor).astype(BF16)
            wave[n, pl.ds(frame + start, CHUNK), :] = (im * factor).astype(BF16)

    def update(n):
        for start in range(0, frame, CHUNK):
            rows = pl.ds(start, CHUNK)
            re, im = field[n, rows, :frame], field[n, rows, frame:]
            p_re, p_im = probe_ref[0, rows, :], probe_ref[1, rows, :]
            o_re, o_im = patch[n, 0, rows, :].astype(F32), patch[n, 1, rows, :].astype(F32)
            steps = (p_re * re + p_im * im, p_re * im - p_im * re)
            for plane in range(2):
                pieces = [tile_of(steps[plane], t) for t in range(tiles)]
                rolled = [turned(piece) for piece in pieces]
                zero = jnp.zeros_like(pieces[0])
                moved = []
                for t in range(tiles + 1):
                    before = rolled[t - 1] if t > 0 else zero
                    here = rolled[t] if t < tiles else zero
                    moved.append(
                        jnp.where(odd[n], jnp.where(low, before, here), pieces[t] if t < tiles else zero)
                    )
                total[window(n, plane, start)] += jnp.concatenate(moved, axis=1)
            grads[0, rows, :] += o_re * re + o_im * im
            grads[1, rows, :] += o_re * im - o_im * re
            grads[2, rows, :] += (o_re * o_re + o_im * o_im) * live[n]

    stages = (
        exit_wave,
        lambda n: left_product(n, plus_ref),
        lambda n: right_product(n, minus_ref),
        change,
        lambda n: left_product(n, minus_ref),
        lambda n: right_product(n, plus_ref),
        update,
    )
    groups = [range(n, min(n + GROUP, count)) for n in range(0, count, GROUP)]
    for time in range(len(stages) + STAGGER * (len(groups) - 1)):
        for place in reversed(range(len(groups))):
            if 0 <= time - STAGGER * place < len(stages):
                for n in groups[place]:
                    stages[time - STAGGER * place](n)

    part_frame = frame // 2
    for who, l_ref, r_ref, g_ref in ((1 - mode, lsend_ref, rsend_ref, gsend_ref), (mode, lkeep_ref, rkeep_ref, gkeep_ref)):
        upper = pl.ds(pl.multiple_of(who * mid, mid), mid)
        lower = pl.ds(pl.multiple_of(tile_rows + who * part, 32), part)
        l_ref[:, :mid, :] = total[:, upper, :tile_cols]
        l_ref[:, mid:, :] = total[:, lower, :tile_cols]
        for plane in range(2):
            right = jnp.concatenate([total[plane, upper, tile_cols:], total[plane, lower, tile_cols:]], axis=0)
            r_ref[plane] = folded(right[:, :LANES], right[:, LANES:])
        g_ref[...] = grads[:, pl.ds(pl.multiple_of(who * part_frame, part_frame), part_frame), :]


def after_mode_kernel(rkeep, rrecv, gkeep, grecv, xsend_ref, g_ref, gsend_ref, w_ref, wsend_ref):
    encode_to(xsend_ref, [rkeep[plane] + rrecv[plane] for plane in range(2)])
    sums = [gkeep[plane] + grecv[plane] for plane in range(3)]
    g_ref[0], g_ref[1] = encode_to(gsend_ref, sums[:2])
    (w_ref[...],) = encode_to(wsend_ref, sums[2:])


def joined_kernel(g, grecv, w, wrecv, sums_ref, send_ref):
    got = decode(grecv, 2, *w.shape) + decode(wrecv, 1, *w.shape)
    sums = [g[0] + got[0], g[1] + got[1], w[...] + got[2]]
    sums_ref[0], sums_ref[1], sums_ref[2] = encode_to(send_ref, sums)


def split_kernel(sums, recv, g_ref, gsend_ref, w_ref, wsend_ref):
    total = [sums[plane] + got for plane, got in enumerate(decode(recv, 3, *sums.shape[1:]))]
    g_ref[0], g_ref[1] = encode_to(gsend_ref, total[:2])
    (w_ref[...],) = encode_to(wsend_ref, total[2:])


def again_kernel(sums, recv, sums_ref, send_ref):
    total = [sums[plane] + got for plane, got in enumerate(decode(recv, 3, *sums.shape[1:]))]
    sums_ref[0], sums_ref[1], sums_ref[2] = encode_to(send_ref, total)


def from_left_kernel(lkeep, lrecv, xrecv, tile_ref, rowsend_ref):
    rows = tile_ref.shape[1]
    came = jnp.where(lax.axis_index("col") > 0, 1.0, 0.0)
    below = []
    for plane, code in enumerate(decode(xrecv, 2, lkeep.shape[1] * 3 // 2, LANES)):
        got = unfolded(code) * came
        frame = got.shape[1]
        tile_ref[plane, :, :frame] = lkeep[plane, :rows, :frame] + lrecv[plane, :rows, :frame] + got[:rows]
        tile_ref[plane, :, frame:] = lkeep[plane, :rows, frame:] + lrecv[plane, :rows, frame:]
        near = lkeep[plane, rows:, :frame] + lrecv[plane, rows:, :frame] + got[rows:]
        far = lkeep[plane, rows:, frame:] + lrecv[plane, rows:, frame:]
        below.append(jnp.concatenate([near, far], axis=1))
    encode_to(rowsend_ref, below)


def from_above_kernel(rowrecv, rows_ref, spill_ref):
    got = decode(rowrecv, 2, *rows_ref.shape[1:])
    came = jnp.where(lax.axis_index("row") > 0, 1.0, 0.0)
    over = spill_ref.shape[1]
    for plane in range(2):
        rows_ref[plane] = got[plane] * came
        spill_ref[plane] = got[plane][:over] * came


def object_kernel(object_ref, tile, rows, spilled, probe_ref, out_ref):
    mode = lax.axis_index("mode")
    mid, part = tile.shape[1], rows.shape[1]
    over = mid - part
    power = probe_ref[0] * probe_ref[0] + probe_ref[1] * probe_ref[1]
    scale = 1.0 / (jnp.max(power, keepdims=True) + EPSILON)
    for who in range(2):

        @pl.when(mode == who)
        def _(who=who):
            for plane in range(2):
                for start in range(0, mid, CHUNK):
                    step = tile[plane, start : start + CHUNK, :]
                    if who == 0:
                        step += rows[plane, start : start + CHUNK, :] if start < part else spilled[plane, start - part :, :]
                    elif start < part - over:
                        step += rows[plane, start + over : start + over + CHUNK, :]
                    old = object_ref[who * mid + start : who * mid + start + CHUNK, plane, :]
                    out_ref[start : start + CHUNK, plane, :] = old + step * scale


def probe_kernel(g, grecv, w, wrecv, step_ref):
    weight = w[...] + decode(wrecv, 1, *w.shape)[0] + REGULARIZER
    got = decode(grecv, 2, *w.shape)
    for plane in range(2):
        step_ref[plane] = (g[plane] + got[plane]) / weight


def put_half(who, probe_ref, step, out_ref, block, arrived):
    rows = step.shape[1]
    place = pl.ds(pl.multiple_of(who * rows, rows), rows)
    for plane in range(2):
        block[:, plane, :] = probe_ref[place, plane, :] + step[plane]
    copy = pltpu.make_async_copy(block, out_ref.at[place], arrived)
    copy.start()
    copy.wait()


def probe_mine_kernel(probe_ref, step, out_ref, block, arrived):
    put_half(lax.axis_index("mode"), probe_ref, step, out_ref, block, arrived)


def probe_other_kernel(probe_ref, step, before_ref, out_ref, block, arrived):
    del before_ref
    put_half(1 - lax.axis_index("mode"), probe_ref, step, out_ref, block, arrived)


def moved_along(value, axis, steps):
    count = lax.axis_size(axis)
    if count == 2:
        return swapped(value, axis, 1)
    first, last = (max(0, -steps), min(count, count - steps))
    return lax.ppermute(value, axis, [(source, source + steps) for source in range(first, last)])


def swapped(value, axis, distance):
    count = lax.axis_size(axis)
    return lax.ppermute(value, axis, [(source, source ^ distance) for source in range(count)])


def frames(row_offset, col_offset, counts, own, pieces, probe, amplitudes, plus, minus):
    _, tile_rows, tile_cols = own.shape
    frame = probe.shape[1]
    halo = frame - STEP
    held = (tile_rows + halo) // 2
    count = amplitudes.shape[0]
    l_shape = shape((2, held, tile_cols), F32)
    r_shape = shape((2, held * 3 // 2, LANES), F32)
    g_shape = shape((3, frame // 2, frame), F32)
    return vmem_call(
        frames_kernel,
        (l_shape, l_shape, r_shape, r_shape, g_shape, g_shape),
        row_offset, col_offset, counts, own, *pieces, probe, amplitudes, plus, minus,
        smem=3,
        scratch=[
            pltpu.VMEM((2, tile_rows + halo, tile_cols + frame), BF16),
            pltpu.VMEM((count, 2, frame, frame), BF16),
            pltpu.VMEM((count, 2 * frame, frame), BF16),
            pltpu.VMEM((count, frame, 2 * frame), BF16),
            pltpu.VMEM((count, frame, 2 * frame), F32),
            pltpu.VMEM((2, tile_rows + halo, tile_cols + frame), F32),
            pltpu.VMEM((3, frame, frame), F32),
        ],
        flops=4 * 32 * frame**3,
        name="frames",
    )


def body(object_field, probe_field, amplitudes, row_offset, col_offset, counts):
    tile_rows, _, tile_cols = object_field.shape
    frame = probe_field.shape[0]
    halo = frame - STEP
    part, mid = halo // 2, tile_rows // 2
    rows_count, cols_count = lax.axis_size("row"), lax.axis_size("col")
    mode = lax.axis_index("mode")
    plus, minus = dft_tables(frame)

    def planar(block):
        return jnp.transpose(block.astype(BF16), (1, 0, 2))

    r_send = planar(lax.dynamic_slice_in_dim(object_field, mode * part, part, 0))
    corner = r_send[:, :, :halo]
    thin = corner[:, :, LANES:]
    thin = jnp.concatenate([thin[:, : part // 2], thin[:, part // 2 :]], axis=2)
    d_send = jnp.concatenate([corner[:, :, :LANES], thin], axis=1)
    object_later, r_send, d_send = lax.optimization_barrier((object_field, r_send, d_send))
    x_send = planar(lax.dynamic_slice_in_dim(object_later[:, :, :halo], mode * mid, mid, 0))
    x_send, x_last = lax.optimization_barrier((x_send[:1], x_send[1:]))
    diagonal = []
    for r in range(1, rows_count):
        for c in range(1, cols_count):
            here = r * cols_count + c
            diagonal.append((here, here - cols_count - 1))
    r_mine = moved_along(r_send, "row", -1)
    d_mine = lax.ppermute(d_send, ("row", "col"), diagonal)
    x_mine, x_last = moved_along(x_send, "col", -1), moved_along(x_last, "col", -1)
    r_mine, d_mine, x_mine, x_last = lax.optimization_barrier((r_mine, d_mine, x_mine, x_last))
    x_mine = jnp.concatenate([x_mine, x_last], axis=0)
    r_other, d_other, x_other = (swapped(v, "mode", 1) for v in (r_mine, d_mine, x_mine))
    own = planar(object_later)
    probe = jnp.transpose(probe_field, (1, 0, 2))

    pieces = (r_mine, r_other, x_mine, x_other, d_mine, d_other)
    lkeep, lsend, rkeep, rsend, gkeep, gsend = frames(
        row_offset, col_offset, counts, own, pieces, probe, amplitudes, plus, minus
    )
    held = mid + part
    rrecv = swapped(rsend, "mode", 1)
    grecv = swapped(gsend, "mode", 1)
    rrecv, grecv, lsend = lax.optimization_barrier((rrecv, grecv, lsend))
    lrecv = swapped(lsend, "mode", 1)

    quarter = frame // 2
    g_out = (shape((2, quarter, frame), F32), code_shape(2, quarter, frame))
    w_out = (shape((quarter, frame), F32), code_shape(1, quarter, frame))
    all_out = (shape((3, quarter, frame), F32), code_shape(3, quarter, frame))
    row_steps = [("row", 1 << k) for k in range(rows_count.bit_length() - 1)]
    col_steps = [("col", 1 << k) for k in range(cols_count.bit_length() - 1)]

    xsend, g, gcode, w, wcode = vmem_call(
        after_mode_kernel, (code_shape(2, held * 3 // 2, LANES), *g_out, *w_out),
        rkeep, rrecv, gkeep, grecv, name="after_mode",
    )
    xrecv = moved_along(xsend, "col", 1)
    gother, wother = swapped(gcode, *row_steps[0]), swapped(wcode, *row_steps[1])
    sums, code = vmem_call(joined_kernel, all_out, g, gother, w, wother, name="joined")
    xrecv, code = lax.optimization_barrier((xrecv, code))
    came = swapped(code, *col_steps[0])
    tile, rowsend = vmem_call(
        from_left_kernel,
        (shape((2, mid, tile_cols), F32), code_shape(2, part, tile_cols)),
        lkeep, lrecv, xrecv, name="from_left",
    )
    rowrecv = moved_along(rowsend, "row", 1)
    for step in row_steps[2:] + col_steps[1:]:
        sums, code = vmem_call(again_kernel, all_out, sums, came, name="again")
        came = swapped(code, *step)
    g, gcode, w, wcode = vmem_call(
        split_kernel, (*g_out, w_out[0], code_shape(1, quarter, frame, tail=WTAIL)), sums, came, name="split"
    )
    gother, wother = swapped(gcode, *row_steps[1]), swapped(wcode, *row_steps[0])

    rowrecv, w = lax.optimization_barrier((rowrecv, w))
    rows, spill = vmem_call(
        from_above_kernel,
        (shape((2, part, tile_cols), F32), shape((2, mid - part, tile_cols), F32)), rowrecv, name="from_above",
    )
    spilled = swapped(spill, "mode", 1)
    (object_new,) = vmem_call(
        object_kernel, (shape((mid, 2, tile_cols), F32),), object_field, tile, rows, spilled, probe, name="object"
    )
    object_new, gother = lax.optimization_barrier((object_new, gother))
    (step,) = vmem_call(probe_kernel, (shape((2, quarter, frame), F32),), g, gother, w, wother, name="probe")
    other = swapped(step, "mode", 1)
    out = (shape(probe_field.shape, F32),)
    scratch = [pltpu.VMEM((quarter, 2, frame), F32), pltpu.SemaphoreType.DMA]
    (half_new,) = vmem_call(
        probe_mine_kernel, out, probe_field, step, far_out=True, scratch=scratch, name="probe_mine"
    )
    (probe_new,) = vmem_call(
        probe_other_kernel, out, probe_field, other, half_new,
        far=(2,), far_out=True, into=2, scratch=scratch, name="probe_other",
    )
    return (object_new, probe_new)


def solution(mesh):
    placed = (
        P(("groups", "row"), None, "col"),
        P("groups", None, None),
        P(("groups", "row", "col", "mode"), None, None),
        P(("groups", "row", "col", "mode")),
        P(("groups", "row", "col", "mode")),
        P(("groups", "row", "col", "mode")),
    )
    return jax.shard_map(
        body,
        mesh=mesh,
        in_specs=placed,
        out_specs=(P(("groups", "row", "mode"), None, "col"), P("groups", None, None)),
        check_vma=False,
    )
```
